32 devices in a mesh: ens: 2 (over y), lon: 4 (over z), lat: 2 (over x), lev: 2 (over core).
Axes of the slice: x: 2, y: 2, z: 4, core: 2. Of those that a mesh axis runs over, the one named last changes fastest.
Arguments:
- fields: bfloat16 [32, 8, 32, 512], P('lev', 'ens', 'lat', 'lon'), parts along dimension 1, may hold values from -6 to 6
- arrival_cot: bfloat16 [32, 8, 32, 512], P('lev', 'ens', 'lat', 'lon'), parts along dimension 1, may hold values from -6 to 6
- weights: bfloat16 [2, 32, 4, 4, 4, 128], P('lev', 'lat', 'lon', 'ens'), parts along dimension 3, may hold values from -2 to 2
- departures: int32 [2, 32, 4, 4, 3], P('lev', 'lat', None, 'ens'), parts along dimension 3, may hold values from -1 to 15, as said below
- counts: int32 [2, 32, 8], P('lev', 'lat', 'ens'), parts along dimension 2, may hold values from 1 to 2
Outputs:
- source_cot: float32 [32, 8, 32, 512], P('lev', 'ens', 'lat', 'lon'), parts along dimension 1
- weight_cot: bfloat16 [2, 32, 4, 4, 4, 128], P('lev', 'lat', 'lon', 'ens'), parts along dimension 3
The draws below stay inside these ranges and needn't reach their ends.
There are 2 independent parts, one for each index of `ens`. The reference program is written for one: setup_inputs(seed, part) draws one part's arguments, and reference() takes and returns one part's arrays. A program takes and returns all parts, laid end to end along the dimension named above; each array names one. Nothing has to cross between parts.
Inputs may be any that keep to these rules, and one draw needn't show every extreme that they name: `departures`: entry k of an arrival row block is used only for k below its count. A used entry names the arrival's own band (shift 0), one of the last 2 rows of the band above (shift -1) or one of the first 2 rows of the band below (shift 1), never a band beyond the first or last. Outside the first and last band a used entry names the arrival tile or one of its two neighbours on the loop of tiles. Over the used entries of one arrival tile, band and level group, no owner tile is named more than 11 times, and outside the first and last band the arrival's own tile is named exactly 11 times.
All inputs are finite; a program needn't handle non-finite values.
Results may differ from the reference program's by a relative error of at most 0.008.
Values may be sent and summed in bfloat16 or wider, within the bound.
No kernel may reach another device: no remote copies, remote signals or barrier semaphores. Data moves between devices by JAX's collectives and lax.ppermute only.
A program may use at most 64 MiB of HBM per device.

```python
import jax
import jax.numpy as jnp
from jax import lax

FIELDS = 4
LEV_DEV = 16
ROWS = 16
COLS = 128
KMAX = 2
HR = 2
TAPS = 4
TILES = 4
BANDS = 2
LEVGRP = 2
NLAT = 32
NLON = 512
LEVELS = 32
CAP = 11


def departure_table(key):
    key = jax.random.fold_in(key, 11)
    key_count, key_row = jax.random.split(key)
    band_index = jnp.arange(BANDS, dtype=jnp.int32)
    polar = jnp.abs(2 * band_index - (BANDS - 1))
    limit = 30 + 40 * polar // (BANDS - 1)
    chance = jax.random.randint(key_count, (LEVGRP, BANDS, ROWS, TILES), 0, 100, dtype=jnp.int32)
    extra = (chance < limit[None, :, None, None]).astype(jnp.int32)
    number = 1 + extra * (KMAX - 1)
    slot_index = jnp.arange(KMAX, dtype=jnp.int32)
    usable = slot_index[None, None, None, None, :] < number[..., None]
    flat_used = jnp.transpose(usable, (0, 1, 3, 2, 4)).reshape(LEVGRP, BANDS, TILES, ROWS * KMAX).astype(jnp.int32)
    used_rank = jnp.maximum(jnp.cumsum(flat_used, axis=-1) - 1, 0)
    polar_band = (band_index == 0) | (band_index == BANDS - 1)
    owner_step = jnp.where(polar_band[None, :, None, None], used_rank % TILES, used_rank // CAP)
    step_off = jnp.where(owner_step % 2 == 1, (owner_step + 1) // 2, -(owner_step // 2))
    arrival = jnp.arange(TILES, dtype=jnp.int32)[None, None, :, None]
    owner_tile = (arrival + step_off) % TILES
    owner_tile = jnp.where(flat_used == 1, owner_tile, arrival + 0 * step_off)
    owner_tile = owner_tile.reshape(LEVGRP, BANDS, TILES, ROWS, KMAX)
    owner_tile = jnp.transpose(owner_tile, (0, 1, 3, 2, 4))
    lower = jnp.where(band_index == 0, HR, 0)
    upper = jnp.where(band_index == BANDS - 1, ROWS + HR, ROWS + 2 * HR)
    ext_row = jax.random.randint(key_row, (LEVGRP, BANDS, ROWS, TILES, KMAX), lower[None, :, None, None, None], upper[None, :, None, None, None], dtype=jnp.int32)
    band_shift = (ext_row >= HR + ROWS).astype(jnp.int32) - (ext_row < HR).astype(jnp.int32)
    row_offset = ext_row - HR - band_shift * ROWS
    table = jnp.stack([owner_tile, band_shift, row_offset], -1).reshape(LEVGRP, NLAT, TILES, KMAX, 3)
    return (table.astype(jnp.int32), number.reshape(LEVGRP, NLAT, TILES).astype(jnp.int32))


def draw_departures(key, part):
    return departure_table(key)[0]


def draw_counts(key, part):
    return departure_table(key)[1]


def steps_of(key, dims, cuts, low, top_value):
    level = 1.0
    for position, blocks in cuts:
        steps = jax.random.uniform(jax.random.fold_in(jax.random.fold_in(key, 6), position), (blocks,), jnp.float32, low / len(cuts), top_value / len(cuts))
        level = level * jnp.repeat(jnp.exp(steps), dims[position] // blocks).reshape((-1,) + (1,) * (len(dims) - 1 - position))
    return level


def noise(key, shape, deviation, most, cuts=(), held_as=jnp.bfloat16):
    drawn = jax.random.normal(key, shape, jnp.float32) * deviation
    if len(cuts) > 0:
        drawn = steps_of(key, shape, cuts, -0.22, 0.18) * drawn
    return jnp.clip(drawn, min=-most, max=most).astype(held_as)


def setup_inputs(seed: int = 0, part: int = 0) -> dict:
    splits = jax.random.split(jax.random.key(seed), 6)
    part_splits = jax.random.split(jax.random.fold_in(splits[5], part), 6)
    return {
        "fields": noise(part_splits[0], (LEVELS, FIELDS, NLAT, NLON), 1.0, 6.0, ((0, 2), (2, 2), (3, 4))),
        "arrival_cot": noise(part_splits[1], (LEVELS, FIELDS, NLAT, NLON), 1.0, 6.0, ((0, 2), (2, 2), (3, 4))),
        "weights": noise(part_splits[2], (LEVGRP, NLAT, TILES, KMAX, TAPS, COLS), (TAPS * KMAX) ** -0.5, 2.0, ((0, 2), (1, 2), (2, 4))),
        "departures": draw_departures(jax.random.fold_in(jax.random.fold_in(splits[5], part), 71), part),
        "counts": draw_counts(jax.random.fold_in(jax.random.fold_in(splits[5], part), 71), part),
    }


source_gain = 1.0


def one_group(packed):
    group_fields, group_cot, group_weights, group_lists, group_counts = packed
    owner_tile = group_lists[..., 0].astype(jnp.int32)
    band_shift = group_lists[..., 1].astype(jnp.int32)
    row_offset = group_lists[..., 2].astype(jnp.int32)
    band_index = (jnp.arange(NLAT, dtype=jnp.int32) // ROWS)[:, None, None]
    src_row = ((band_index + band_shift) * ROWS + row_offset).astype(jnp.int32)
    usable = jnp.arange(KMAX, dtype=jnp.int32)[None, None, :] < group_counts[..., None]
    blocks = group_fields[:, src_row, owner_tile, :]
    blocks = jnp.where(usable[None, ..., None], blocks, jnp.zeros((), blocks.dtype))
    mixing = group_weights.astype(jnp.float32)
    tap_cols = jnp.clip(jnp.arange(COLS, dtype=jnp.int32)[None, :] + jnp.arange(TAPS, dtype=jnp.int32)[:, None] - 1, 0, COLS - 1).astype(jnp.int32)
    channels = group_fields.shape[0]
    interp = jnp.zeros((channels, NLAT, TILES, COLS), jnp.float32)
    for tap in range(TAPS):
        shifted = blocks[..., tap_cols[tap]].astype(jnp.float32)
        interp = interp + jnp.einsum('crtka,rtka->crta', shifted, mixing[:, :, :, tap, :])
    scaled = (group_cot.astype(jnp.float32) * (1.0 + source_gain * (1.0 - jnp.tanh(interp) ** 2))).astype(jnp.bfloat16)
    scaled_f = scaled.astype(jnp.float32)
    term = jnp.zeros((channels, NLAT, TILES, KMAX, COLS), jnp.float32)
    grads = []
    for tap in range(TAPS):
        term = term.at[..., tap_cols[tap]].add(scaled_f[:, :, :, None, :] * mixing[None, :, :, :, tap, :])
        shifted = blocks[..., tap_cols[tap]].astype(jnp.float32)
        grads.append(jnp.einsum('crtka,crta->rtka', shifted, scaled_f))
    term = jnp.where(usable[None, ..., None], term, 0.0).astype(jnp.bfloat16)
    weight_grad = jnp.stack(grads, axis=3).astype(jnp.bfloat16)
    summed = jnp.zeros((channels, NLAT, TILES, COLS), jnp.float32)
    summed = summed.at[:, src_row, owner_tile, :].add(term.astype(jnp.float32))
    return summed, weight_grad


def reference(fields, arrival_cot, weights, departures, counts):
    channels = LEV_DEV * FIELDS
    group_fields = fields.reshape(LEVGRP, channels, NLAT, TILES, COLS)
    group_cot = arrival_cot.reshape(LEVGRP, channels, NLAT, TILES, COLS)
    summed, weight_grad = lax.map(one_group, (group_fields, group_cot, weights, departures, counts))
    source_cot = summed.reshape(LEVELS, FIELDS, NLAT, NLON)
    return source_cot, weight_grad
```

```python
import functools

import jax
import jax.numpy as jnp
from jax import lax
from jax.experimental import pallas as pl
from jax.experimental.pallas import tpu as pltpu
from jax.sharding import PartitionSpec as P

HR = 2
CAP = 11
STRIDE = 16
SHIFT = 8
BF16 = jnp.bfloat16
F32 = jnp.float32
VMEM = pltpu.VMEM
SMEM = pltpu.SMEM


def whole(space):
    return pl.BlockSpec(memory_space=space)


def wrap(value, size):
    return jnp.where(value < 0, value + size, value)


def prepare_kernel(tiles, per_row, code_ref, fields_ref, rows_ref, send_ref, loc_ref, wide, taken):
    rows, channels, _ = rows_ref.shape
    me = lax.axis_index("lon")
    dump = rows + 2 * HR
    wide[...] = fields_ref[...].astype(F32)
    for r in range(rows):
        rows_ref[r] = wide[pl.ds(r, channels, stride=rows), :].astype(BF16)

    def serve(a, _):
        base = wrap(a - me, tiles) * STRIDE
        filled = jnp.int32(0)
        for r in range(rows):
            for k in range(per_row):
                code = code_ref[(r * tiles + a) * per_row + k]
                send_ref[base + filled] = code & ((1 << SHIFT) - 1)
                filled = filled + jnp.where((code >> SHIFT) == me, 1, 0)
        for s in range(CAP):
            send_ref[base + s] = jnp.where(s < filled, send_ref[base + s], dump)
        return 0

    lax.fori_loop(0, tiles, serve, 0)
    for d in range(tiles + 1):
        taken[d] = 0

    def place(r, _):
        for k in range(per_row):
            code = code_ref[(r * tiles + me) * per_row + k]
            owner = code >> SHIFT
            used = owner >= 0
            d = jnp.where(used, wrap(me - owner, tiles), tiles)
            slot = taken[d]
            taken[d] = slot + 1
            loc_ref[r * per_row + k] = jnp.where(used, d * CAP + slot, tiles * CAP)
        return 0

    lax.fori_loop(0, rows, place, 0)


def pack_kernel(tiles, send_ref, rows_ref, before_ref, after_ref, *rest):
    outs, (ext, wide) = rest[:tiles], rest[tiles:]
    rows, channels, _ = rows_ref.shape
    ext[HR : HR + rows] = rows_ref[...]
    for start, halo in ((0, before_ref), (HR + rows, after_ref)):
        wide[...] = halo[...].astype(F32)
        for h in range(HR):
            ext[start + h] = wide[pl.ds(h, channels, stride=HR), :].astype(BF16)
    for d in range(tiles):
        for s in range(CAP):
            outs[d][s] = ext[send_ref[d * STRIDE + s]]


def arrival_kernel(cot_ref, taps_ref, cot_rows_ref, folded_ref, wide):
    rows, channels, cols = cot_rows_ref.shape
    wide[...] = cot_ref[...].astype(F32)
    for r in range(rows):
        cot_rows_ref[r] = wide[pl.ds(r, channels, stride=rows), :].astype(BF16)
    w0, w1, w2, w3 = (taps_ref[j] for j in range(4))
    cell = lax.broadcasted_iota(jnp.int32, w0.shape, 1)
    first, last, late = cell == 0, cell == cols - 1, cell == cols - 2
    folded_ref[0] = jnp.where(first, 0.0, w0)
    folded_ref[1] = w1 + jnp.where(first, w0, 0.0) + jnp.where(last, w2 + w3, 0.0)
    folded_ref[2] = jnp.where(last, 0.0, w2) + jnp.where(late, w3, 0.0)
    folded_ref[3] = jnp.where(last | late, 0.0, w3)


def compute_kernel(tiles, per_row, loc_ref, folded_ref, cot_ref, *rest):
    arrived, rest = rest[:tiles], rest[tiles:]
    outs, rest = rest[:tiles], rest[tiles:]
    grad_ref, blocks, terms = rest
    rows, channels, cols = cot_ref.shape
    part = min(channels, 32)
    for d in range(tiles):
        blocks[d * CAP : (d + 1) * CAP] = arrived[d][...]
    blocks[tiles * CAP] = jnp.zeros((channels, cols), BF16)

    def row(r, _):
        index = [loc_ref[r * per_row + k] for k in range(per_row)]
        mix = [
            [folded_ref[j, pl.ds(r * per_row + k, 1), :] for j in range(4)] for k in range(per_row)
        ]
        grads = [[jnp.zeros((8, cols), F32) for _ in range(4)] for _ in range(per_row)]
        for lo in range(0, channels, part):
            shifted = []
            interp = jnp.zeros((part, cols), F32)
            for k in range(per_row):
                block = blocks[index[k], lo : lo + part].astype(F32)
                moved = [
                    pltpu.roll(block, 1, 1),
                    block,
                    pltpu.roll(block, cols - 1, 1),
                    pltpu.roll(block, cols - 2, 1),
                ]
                for j in range(4):
                    interp = interp + moved[j] * mix[k][j]
                shifted.append(moved)
            bent = jnp.tanh(interp)
            scaled = cot_ref[r, lo : lo + part].astype(F32) * (2.0 - bent * bent)
            scaled = scaled.astype(BF16).astype(F32)
            for k in range(per_row):
                pieces = [scaled * mix[k][j] for j in range(4)]
                term = (
                    pieces[1]
                    + pltpu.roll(pieces[0], cols - 1, 1)
                    + pltpu.roll(pieces[2], 1, 1)
                    + pltpu.roll(pieces[3], 2, 1)
                )
                terms[index[k], lo : lo + part] = term.astype(BF16)
                for j in range(4):
                    product = (shifted[k][j] * scaled).reshape(part // 8, 8, cols)
                    grads[k][j] = grads[k][j] + jnp.sum(product, axis=0)
        for k in range(per_row):
            for j in range(4):
                grad_ref[r, k * 4 + j : k * 4 + j + 1, :] = jnp.sum(grads[k][j], axis=0, keepdims=True)
        return 0

    lax.fori_loop(0, rows, row, 0)
    for d in range(tiles):
        outs[d][...] = terms[d * CAP : (d + 1) * CAP]


def gather_kernel(tiles, send_ref, *rest):
    returned, (rows_ref, first_ref, last_ref, total) = rest[:tiles], rest[tiles:]
    rows = rows_ref.shape[0]
    total[...] = jnp.zeros_like(total)
    for d in range(tiles):
        for s in range(CAP):
            at = send_ref[d * STRIDE + s]
            total[at] = total[at] + returned[d][s].astype(F32)
    rows_ref[...] = total[HR : HR + rows]
    first_ref[...] = total[0:HR].astype(BF16)
    last_ref[...] = total[HR + rows : HR + rows + HR].astype(BF16)


def finish_kernel(bands, rows_ref, above_ref, below_ref, out_ref):
    rows, channels, _ = rows_ref.shape
    band = lax.axis_index("lat")
    has_above = jnp.where(band > 0, 1, 0)
    has_below = jnp.where(band < bands - 1, 1, 0)
    for r in range(rows):
        value = rows_ref[r]
        if r < HR:
            value = value + jnp.where(has_above == 1, above_ref[r].astype(F32), 0.0)
        if r >= rows - HR:
            value = value + jnp.where(has_below == 1, below_ref[r - rows + HR].astype(F32), 0.0)
        out_ref[pl.ds(r, channels, stride=rows), :] = value


def swap_lat(to_above, to_below, bands):
    band = lax.axis_index("lat")
    if bands == 2:
        sent = jnp.where(band == 0, to_below, to_above)
        got = lax.ppermute(sent, "lat", [(0, 1), (1, 0)])
        return got, got
    down = [(i, i + 1) for i in range(bands - 1)]
    up = [(i + 1, i) for i in range(bands - 1)]
    return lax.ppermute(to_below, "lat", down), lax.ppermute(to_above, "lat", up)


def local(fields, arrival_cot, weights, departures, counts):
    lev_dev, field_count, rows, cols = fields.shape
    channels = lev_dev * field_count
    tiles = lax.axis_size("lon")
    bands = lax.axis_size("lat")
    my_tile = lax.axis_index("lon")
    per_row, taps = weights.shape[3], weights.shape[4]
    ext = rows + 2 * HR
    params = pltpu.CompilerParams(vmem_limit_bytes=48 * 1024 * 1024)

    def call(kernel, out_shape, in_specs, out_specs, scratch=(), name=None):
        return pl.pallas_call(
            kernel,
            out_shape=out_shape,
            in_specs=in_specs,
            out_specs=out_specs,
            scratch_shapes=list(scratch),
            compiler_params=params,
            name=name,
        )

    def array(shape, dtype):
        return jax.ShapeDtypeStruct(shape, dtype)

    to_above = fields[:, :, :HR].reshape(channels * HR, cols)
    to_below = fields[:, :, rows - HR :].reshape(channels * HR, cols)
    before, after = swap_lat(to_above, to_below, bands)

    lists = departures.reshape(rows, tiles, per_row, 3)
    number = counts.reshape(rows, tiles)
    usable = jnp.arange(per_row, dtype=jnp.int32)[None, None, :] < number[..., None]
    ext_row = HR + lists[..., 1] * rows + lists[..., 2]
    code = jnp.where(usable, (lists[..., 0] << SHIFT) + ext_row, -1).reshape(-1)

    row_blocks, send_rows, places = call(
        functools.partial(prepare_kernel, tiles, per_row),
        (
            array((rows, channels, cols), BF16),
            array((tiles * STRIDE,), jnp.int32),
            array((rows * per_row,), jnp.int32),
        ),
        [whole(SMEM), whole(VMEM)],
        (whole(VMEM), whole(SMEM), whole(SMEM)),
        [VMEM((channels * rows, cols), F32), SMEM((tiles + 1,), jnp.int32)],
        "prepare",
    )(code, fields.reshape(channels * rows, cols))

    slots = array((CAP, channels, cols), BF16)
    packed = call(
        functools.partial(pack_kernel, tiles),
        (slots,) * tiles,
        [whole(SMEM), whole(VMEM), whole(VMEM), whole(VMEM)],
        (whole(VMEM),) * tiles,
        [VMEM((ext + 1, channels, cols), BF16), VMEM((channels * HR, cols), F32)],
        "pack",
    )(send_rows, row_blocks, before, after)

    def moved(parts, sign):
        out = [parts[0]]
        for d in range(1, tiles):
            route = [(i, (i + sign * d) % tiles) for i in range(tiles)]
            out.append(lax.ppermute(parts[d], "lon", route))
        return out

    arrived = moved(packed, 1)

    mine = lax.dynamic_index_in_dim(usable, my_tile, 1, keepdims=False)
    mixing = weights.reshape(rows, per_row, taps, cols).astype(F32)
    mixing = jnp.where(mine[:, :, None, None], mixing, 0.0)
    mixing = jnp.transpose(mixing, (2, 0, 1, 3)).reshape(taps, rows * per_row, cols)
    cot_rows, folded = call(
        arrival_kernel,
        (array((rows, channels, cols), BF16), array(mixing.shape, F32)),
        [whole(VMEM)] * 2,
        (whole(VMEM),) * 2,
        [VMEM((channels * rows, cols), F32)],
        "arrival",
    )(arrival_cot.reshape(channels * rows, cols), mixing)

    *terms, grads = call(
        functools.partial(compute_kernel, tiles, per_row),
        (slots,) * tiles + (array((rows, per_row * taps, cols), F32),),
        [whole(SMEM)] + [whole(VMEM)] * (2 + tiles),
        (whole(VMEM),) * (tiles + 1),
        [VMEM((tiles * CAP + 1, channels, cols), BF16)] * 2,
        "compute",
    )(places, folded, cot_rows, *arrived)

    returned = moved(terms, -1)

    row_sums, to_above, to_below = call(
        functools.partial(gather_kernel, tiles),
        (
            array((rows, channels, cols), F32),
            array((HR, channels, cols), BF16),
            array((HR, channels, cols), BF16),
        ),
        [whole(SMEM)] + [whole(VMEM)] * tiles,
        (whole(VMEM),) * 3,
        [VMEM((ext + 1, channels, cols), F32)],
        "gather",
    )(send_rows, *returned)

    from_above, from_below = swap_lat(to_above, to_below, bands)

    source = call(
        functools.partial(finish_kernel, bands),
        array((channels * rows, cols), F32),
        [whole(VMEM)] * 3,
        whole(VMEM),
        (),
        "finish",
    )(row_sums, from_above, from_below)

    grads = grads.reshape(rows, per_row, taps, cols)
    g0, g1, g2, g3 = (grads[:, :, j] for j in range(4))
    cell = jnp.arange(cols)[None, None, :]
    g0 = jnp.where(cell == 0, g1, g0)
    g3 = jnp.where(cell == cols - 2, g2, g3)
    g3 = jnp.where(cell == cols - 1, g1, g3)
    g2 = jnp.where(cell == cols - 1, g1, g2)
    weight_grad = jnp.stack([g0, g1, g2, g3], axis=2)
    weight_grad = jnp.where(mine[:, :, None, None], weight_grad, 0.0).astype(BF16)
    return source.reshape(fields.shape), weight_grad.reshape(weights.shape)


def solution(mesh):
    return jax.shard_map(
        local,
        mesh=mesh,
        in_specs=(
            P("lev", "ens", "lat", "lon"),
            P("lev", "ens", "lat", "lon"),
            P("lev", "lat", "lon", "ens", None, None),
            P("lev", "lat", None, "ens", None),
            P("lev", "lat", "ens"),
        ),
        out_specs=(P("lev", "ens", "lat", "lon"), P("lev", "lat", "lon", "ens", None, None)),
        check_vma=False,
    )
```

```python
import functools

import jax
import jax.numpy as jnp
from jax import lax
from jax.experimental import pallas as pl
from jax.experimental.pallas import tpu as pltpu
from jax.sharding import PartitionSpec as P

HR = 2
CAP = 11
EARLY = 3
SHARED = 5
SPARE = CAP - SHARED
SLOTS = EARLY + SHARED + SPARE
STRIDE = 16
TRASH = STRIDE - 2
COUNT = STRIDE - 1
BF16 = jnp.bfloat16
F32 = jnp.float32
VMEM = pltpu.VMEM
SMEM = pltpu.SMEM


def whole(space):
    return pl.BlockSpec(memory_space=space)


def wrap(value, size):
    return jnp.where(value < 0, value + size, value)


def decode(lists_ref, number_ref, r, a, k, rows):
    used = k < number_ref[0, r, a]
    owner = jnp.where(used, lists_ref[0, r, a, k, 0], -1)
    shift = lists_ref[0, r, a, k, 1]
    return owner, HR + shift * rows + lists_ref[0, r, a, k, 2], shift == 0


def prepare_kernel(tiles, bands, per_row, lists_ref, number_ref, fields_ref, *rest):
    rows_ref, send_ref, *rest = rest
    edges = rest[: 1 if bands == 2 else 2]
    early = rest[len(edges) : len(edges) + tiles - 1]
    wide = rest[-1]
    rows, channels, _ = rows_ref.shape
    me = lax.axis_index("lon")
    dump = rows + 2 * HR
    for i in range(tiles * STRIDE):
        send_ref[i] = dump

    def serve(a):
        base = wrap(a - me, tiles) * STRIDE
        near = jnp.int32(0)
        other = jnp.int32(0)
        for r in range(rows):
            for k in range(per_row):
                owner, row, own_band = decode(lists_ref, number_ref, r, a, k, rows)
                hit = owner == me
                ahead = hit & own_band & (near < EARLY)
                slot = jnp.where(ahead, near, EARLY + other)
                send_ref[base + jnp.where(hit, slot, TRASH)] = row
                near = near + jnp.where(ahead, 1, 0)
                other = other + jnp.where(hit, 1, 0) - jnp.where(ahead, 1, 0)
        send_ref[base + COUNT] = other

    if tiles <= 4:
        for a in range(tiles):
            serve(a)
    else:
        pl.loop(0, tiles)(serve)
    wide[...] = fields_ref[...].astype(F32)
    for r in range(rows):
        rows_ref[r] = wide[pl.ds(r, channels, stride=rows), :].astype(BF16)
    if bands == 2:
        start = jnp.where(lax.axis_index("lat") == 0, rows - HR, 0)
        edges[0][...] = rows_ref[pl.ds(start, HR)]
    else:
        edges[0][...] = rows_ref[0:HR]
        edges[1][...] = rows_ref[rows - HR : rows]
    for d in range(1, tiles):
        for s in range(EARLY):
            row = send_ref[d * STRIDE + s]
            early[d - 1][s] = rows_ref[jnp.where(row == dump, 0, row - HR)]


def pack_kernel(tiles, send_ref, rows_ref, before_ref, after_ref, *rest):
    shared, (own, spare, ext) = rest[: tiles - 1], rest[tiles - 1 :]
    rows = rows_ref.shape[0]
    ext[0:HR] = before_ref[...]
    ext[HR : HR + rows] = rows_ref[...]
    ext[HR + rows : HR + rows + HR] = after_ref[...]
    for d in range(1, tiles):
        for s in range(SHARED):
            shared[d - 1][s] = ext[send_ref[d * STRIDE + EARLY + s]]
    for s in range(SLOTS):
        own[s] = ext[send_ref[s]]
    for d in range(1, tiles):

        @pl.when(send_ref[d * STRIDE + COUNT] > SHARED)
        def _():
            for s in range(SPARE):
                spare[d - 1, s] = ext[send_ref[d * STRIDE + EARLY + SHARED + s]]


def arrival_kernel(
    tiles, per_row, lists_ref, number_ref, cot_ref, taps_ref, cot_rows_ref, mix_ref, place_ref, wide, near, other
):
    rows, channels, cols = cot_rows_ref.shape
    me = lax.axis_index("lon")
    for d in range(tiles + 1):
        near[d] = 0
        other[d] = 0

    def place(r):
        for k in range(per_row):
            owner, _, own_band = decode(lists_ref, number_ref, r, me, k, rows)
            used = owner >= 0
            d = jnp.where(used, wrap(me - owner, tiles), tiles)
            ahead = own_band & (near[d] < EARLY)
            slot = d * SLOTS + jnp.where(ahead, near[d], EARLY + other[d])
            place_ref[r * per_row + k] = jnp.where(used, slot, tiles * SLOTS)
            near[d] = near[d] + jnp.where(ahead, 1, 0)
            other[d] = other[d] + jnp.where(ahead, 0, 1)

    pl.loop(0, rows)(place)
    for d in range(tiles):
        place_ref[rows * per_row + d] = other[d]

    wide[...] = cot_ref[...].astype(F32)
    for r in range(rows):
        cot_rows_ref[r] = wide[pl.ds(r, channels, stride=rows), :].astype(BF16)
    w0, w1, w2, w3 = (taps_ref[j] for j in range(4))
    cell = lax.broadcasted_iota(jnp.int32, w0.shape, 1)
    first, last, late = cell == 0, cell == cols - 1, cell == cols - 2
    mix_ref[0] = pltpu.roll(jnp.where(first, 0.0, w0), cols - 1, 1)
    mix_ref[1] = w1 + jnp.where(first, w0, 0.0) + jnp.where(last, w2 + w3, 0.0)
    mix_ref[2] = pltpu.roll(jnp.where(last, 0.0, w2) + jnp.where(late, w3, 0.0), 1, 1)
    mix_ref[3] = pltpu.roll(jnp.where(last | late, 0.0, w3), 2, 1)


def compute_kernel(tiles, per_row, place_ref, mix_ref, cot_ref, own_ref, *rest):
    n = tiles - 1
    early, shared, spare, rest = rest[:n], rest[n : 2 * n], rest[2 * n], rest[2 * n + 1 :]
    own_out, early_out, rest = rest[0], rest[1 : n + 1], rest[n + 1 :]
    shared_out, (spare_out, grad_ref, blocks, terms) = rest[:n], rest[n:]
    rows, channels, cols = cot_ref.shape
    part = min(channels, 32)
    blocks[0:SLOTS] = own_ref[...]
    for d in range(1, tiles):
        base = d * SLOTS
        blocks[base : base + EARLY] = early[d - 1][...]
        blocks[base + EARLY : base + EARLY + SHARED] = shared[d - 1][...]

        @pl.when(place_ref[rows * per_row + d] > SHARED)
        def _():
            blocks[base + EARLY + SHARED : base + SLOTS] = spare[d - 1]

    blocks[tiles * SLOTS] = jnp.zeros((channels, cols), BF16)

    def row(r, _):
        index = [place_ref[r * per_row + k] for k in range(per_row)]
        mix = [[mix_ref[j, pl.ds(r * per_row + k, 1), :] for j in range(4)] for k in range(per_row)]
        for lo in range(0, channels, part):
            block = [blocks[index[k], lo : lo + part].astype(F32) for k in range(per_row)]
            tap = [sum(block[k] * mix[k][j] for k in range(per_row)) for j in range(4)]
            interp = (tap[1] + pltpu.roll(tap[0], 1, 1)) + (
                pltpu.roll(tap[2], cols - 1, 1) + pltpu.roll(tap[3], cols - 2, 1)
            )
            bent = jnp.tanh(interp)
            scaled = cot_ref[r, lo : lo + part].astype(F32) * (2.0 - bent * bent)
            scaled = scaled.astype(BF16).astype(F32)
            moved = [
                pltpu.roll(scaled, cols - 1, 1),
                scaled,
                pltpu.roll(scaled, 1, 1),
                pltpu.roll(scaled, 2, 1),
            ]
            for k in range(per_row):
                term = (moved[0] * mix[k][0] + moved[1] * mix[k][1]) + (
                    moved[2] * mix[k][2] + moved[3] * mix[k][3]
                )
                terms[index[k], lo : lo + part] = term.astype(BF16)
                for j in range(4):
                    at = (r * per_row + k) * 4 + j
                    product = jnp.sum((block[k] * moved[j]).reshape(part // 8, 8, cols), axis=0)
                    grad_ref[at] = product if lo == 0 else grad_ref[at] + product
        return 0

    lax.fori_loop(0, rows, row, 0, unroll=4)
    own_out[...] = terms[0:SLOTS]
    for d in range(1, tiles):
        base = d * SLOTS
        early_out[d - 1][...] = terms[base : base + EARLY]
        shared_out[d - 1][...] = terms[base + EARLY : base + EARLY + SHARED]

        @pl.when(place_ref[rows * per_row + d] > SHARED)
        def _():
            spare_out[d - 1] = terms[base + EARLY + SHARED : base + SLOTS]


def add_own_kernel(send_ref, own_ref, total_ref):
    total_ref[...] = jnp.zeros_like(total_ref)
    for s in range(SLOTS):
        at = send_ref[s]
        total_ref[at] = total_ref[at] + own_ref[s].astype(F32)


def add_shared_kernel(tiles, bands, send_ref, start_ref, spare_ref, *rest):
    shared, (total_ref, *edges) = rest[: tiles - 1], rest[tiles - 1 :]
    ext = total_ref.shape[0] - 1
    total_ref[...] = start_ref[...]
    for d in range(1, tiles):
        for s in range(SHARED):
            at = send_ref[d * STRIDE + EARLY + s]
            total_ref[at] = total_ref[at] + shared[d - 1][s].astype(F32)

        @pl.when(send_ref[d * STRIDE + COUNT] > SHARED)
        def _():
            for s in range(SPARE):
                at = send_ref[d * STRIDE + EARLY + SHARED + s]
                total_ref[at] = total_ref[at] + spare_ref[d - 1, s].astype(F32)

    if bands == 2:
        start = jnp.where(lax.axis_index("lat") == 0, ext - HR, 0)
        edges[0][...] = total_ref[pl.ds(start, HR)].astype(BF16)
    else:
        edges[0][...] = total_ref[0:HR].astype(BF16)
        edges[1][...] = total_ref[ext - HR : ext].astype(BF16)


def finish_kernel(tiles, bands, rows, send_ref, start_ref, above_ref, below_ref, *rest):
    early, (out_ref, total) = rest[: tiles - 1], rest[tiles - 1 :]
    channels = start_ref.shape[1]
    total[...] = start_ref[...]
    for d in range(1, tiles):
        for s in range(EARLY):
            at = send_ref[d * STRIDE + s]
            total[at] = total[at] + early[d - 1][s].astype(F32)
    band = lax.axis_index("lat")
    for r in range(rows):
        value = total[HR + r]
        if r < HR:
            value = value + jnp.where(band > 0, above_ref[r].astype(F32), 0.0)
        if r >= rows - HR:
            value = value + jnp.where(band < bands - 1, below_ref[r - rows + HR].astype(F32), 0.0)
        out_ref[pl.ds(r, channels, stride=rows), :] = value


def swap_lat(edges, bands):
    if bands == 2:
        got = lax.ppermute(edges[0], "lat", [(0, 1), (1, 0)])
        return got, got
    down = [(i, i + 1) for i in range(bands - 1)]
    up = [(i + 1, i) for i in range(bands - 1)]
    return lax.ppermute(edges[1], "lat", down), lax.ppermute(edges[0], "lat", up)


def local(fields, arrival_cot, weights, departures, counts):
    lev_dev, field_count, rows, cols = fields.shape
    channels = lev_dev * field_count
    tiles = lax.axis_size("lon")
    bands = lax.axis_size("lat")
    my_tile = lax.axis_index("lon")
    per_row, taps = weights.shape[3], weights.shape[4]
    ext = rows + 2 * HR
    params = pltpu.CompilerParams(vmem_limit_bytes=48 * 1024 * 1024)

    def call(kernel, out_shape, in_specs, out_specs, scratch=(), name=None):
        return pl.pallas_call(
            kernel,
            out_shape=out_shape,
            in_specs=in_specs,
            out_specs=out_specs,
            scratch_shapes=list(scratch),
            compiler_params=params,
            name=name,
        )

    def array(*shape, dtype=BF16):
        return jax.ShapeDtypeStruct(shape, dtype)

    def moved(parts, sign):
        out = []
        for d, part in enumerate(parts, 1):
            route = [(i, (i + sign * d) % tiles) for i in range(tiles)]
            out.append(lax.ppermute(part, "lon", route))
        return out

    def moved_spare(needed, part, sign):
        def send(part):
            return jnp.stack(moved([part[d] for d in range(tiles - 1)], sign))

        return lax.cond(needed, send, lambda part: part, part)

    partners = tiles - 1
    edge = (array(HR, channels, cols),) * (1 if bands == 2 else 2)
    early_slots = (array(EARLY, channels, cols),) * partners
    shared_slots = (array(SHARED, channels, cols),) * partners
    spare_slots = array(partners, SPARE, channels, cols)
    own_slots = array(SLOTS, channels, cols)

    row_blocks, send_rows, *rest = call(
        functools.partial(prepare_kernel, tiles, bands, per_row),
        (array(rows, channels, cols), array(tiles * STRIDE, dtype=jnp.int32)) + edge + early_slots,
        [whole(SMEM), whole(SMEM), whole(VMEM)],
        (whole(VMEM), whole(SMEM)) + (whole(VMEM),) * (len(edge) + partners),
        [VMEM((channels * rows, cols), F32)],
        "prepare",
    )(departures, counts, fields.reshape(channels * rows, cols))
    edges, early = rest[: len(edge)], rest[len(edge) :]
    early = moved(early, 1)
    before, after = swap_lat(edges, bands)

    lists = departures.reshape(rows, tiles, per_row, 3)
    number = counts.reshape(rows, tiles)
    usable = jnp.arange(per_row, dtype=jnp.int32)[None, None, :] < number[..., None]
    named = usable[..., None] & (lists[..., 0][..., None] == jnp.arange(tiles, dtype=jnp.int32))
    own_band = (lists[..., 1] == 0)[..., None]
    near = jnp.sum(jnp.where(named & own_band, 1, 0), axis=(0, 2))
    far = jnp.sum(jnp.where(named & ~own_band, 1, 0), axis=(0, 2))
    apart = ~jnp.eye(tiles, dtype=bool)
    needed = jnp.any((far + jnp.maximum(near - EARLY, 0) > SHARED) & apart)

    *shared, own, spare = call(
        functools.partial(pack_kernel, tiles),
        shared_slots + (own_slots, spare_slots),
        [whole(SMEM)] + [whole(VMEM)] * 3,
        (whole(VMEM),) * (partners + 2),
        [VMEM((ext + 1, channels, cols), BF16)],
        "pack",
    )(send_rows, row_blocks, before, after)
    shared = moved(shared, 1)
    spare = moved_spare(needed, spare, 1)

    mine = lax.dynamic_index_in_dim(usable, my_tile, 1, keepdims=False)
    mixing = weights.reshape(rows, per_row, taps, cols).astype(F32)
    mixing = jnp.where(mine[:, :, None, None], mixing, 0.0)
    mixing = jnp.transpose(mixing, (2, 0, 1, 3)).reshape(taps, rows * per_row, cols)
    cot_rows, mix, places = call(
        functools.partial(arrival_kernel, tiles, per_row),
        (
            array(rows, channels, cols),
            array(*mixing.shape, dtype=F32),
            array(rows * per_row + tiles, dtype=jnp.int32),
        ),
        [whole(SMEM), whole(SMEM), whole(VMEM), whole(VMEM)],
        (whole(VMEM), whole(VMEM), whole(SMEM)),
        [VMEM((channels * rows, cols), F32)] + [SMEM((tiles + 1,), jnp.int32)] * 2,
        "arrival",
    )(departures, counts, arrival_cot.reshape(channels * rows, cols), mixing)

    own, *rest = call(
        functools.partial(compute_kernel, tiles, per_row),
        (own_slots,)
        + early_slots
        + shared_slots
        + (spare_slots, array(rows * per_row * taps, 8, cols, dtype=F32)),
        [whole(SMEM)] + [whole(VMEM)] * (4 + 2 * partners),
        (whole(VMEM),) * (3 + 2 * partners),
        [VMEM((tiles * SLOTS + 1, channels, cols), BF16)] * 2,
        "compute",
    )(places, mix, cot_rows, own, *early, *shared, spare)
    early, shared, (spare, grads) = rest[:partners], rest[partners : 2 * partners], rest[2 * partners :]

    shared = moved(shared, -1)
    spare = moved_spare(needed, spare, -1)
    early = moved(early, -1)

    sums = array(ext + 1, channels, cols, dtype=F32)
    total = call(add_own_kernel, sums, [whole(SMEM), whole(VMEM)], whole(VMEM), (), "add_own")(
        send_rows, own
    )
    total, *edges = call(
        functools.partial(add_shared_kernel, tiles, bands),
        (sums,) + edge,
        [whole(SMEM)] + [whole(VMEM)] * (2 + partners),
        (whole(VMEM),) * (1 + len(edge)),
        (),
        "add_shared",
    )(send_rows, total, spare, *shared)
    from_above, from_below = swap_lat(edges, bands)
    source = call(
        functools.partial(finish_kernel, tiles, bands, rows),
        array(channels * rows, cols, dtype=F32),
        [whole(SMEM)] + [whole(VMEM)] * (3 + partners),
        whole(VMEM),
        [VMEM((ext + 1, channels, cols), F32)],
        "finish",
    )(send_rows, total, from_above, from_below, *early)

    grads = jnp.sum(grads.reshape(rows, per_row, taps, 8, cols), axis=3)
    g0, g1, g2, g3 = (jnp.roll(grads[:, :, j], 1 - j, axis=-1) for j in range(4))
    cell = jnp.arange(cols)[None, None, :]
    g0 = jnp.where(cell == 0, g1, g0)
    g3 = jnp.where(cell == cols - 2, g2, g3)
    g3 = jnp.where(cell == cols - 1, g1, g3)
    g2 = jnp.where(cell == cols - 1, g1, g2)
    weight_grad = jnp.stack([g0, g1, g2, g3], axis=2)
    weight_grad = jnp.where(mine[:, :, None, None], weight_grad, 0.0).astype(BF16)
    return source.reshape(fields.shape), weight_grad.reshape(weights.shape)


def solution(mesh):
    return jax.shard_map(
        local,
        mesh=mesh,
        in_specs=(
            P("lev", "ens", "lat", "lon"),
            P("lev", "ens", "lat", "lon"),
            P("lev", "lat", "lon", "ens", None, None),
            P("lev", "lat", None, "ens", None),
            P("lev", "lat", "ens"),
        ),
        out_specs=(P("lev", "ens", "lat", "lon"), P("lev", "lat", "lon", "ens", None, None)),
        check_vma=False,
    )
```

```python
import functools

import jax
import jax.numpy as jnp
from jax import lax
from jax.experimental import pallas as pl
from jax.experimental.pallas import tpu as pltpu
from jax.sharding import PartitionSpec as P

HR = 2
CAP = 11
EVEN = 8
EARLY = 4
STRIDE = 32
TRASH = STRIDE - 2
COUNT = STRIDE - 1
PLACES = 16
BF16 = jnp.bfloat16
F32 = jnp.float32
VMEM = pltpu.VMEM
SMEM = pltpu.SMEM


def whole(space):
    return pl.BlockSpec(memory_space=space)


def wrap(value, size):
    return jnp.where(value < 0, value + size, value)


def regions(d, tiles):
    if d == 0:
        return 0, CAP, 0
    early = EARLY if d == tiles // 2 else 0
    shared = EVEN - early
    return early, shared, CAP - shared


def decode(lists_ref, number_ref, r, a, k, rows):
    used = k < number_ref[0, a, r]
    owner = jnp.where(used, lists_ref[0, a, 0, k, r], -1)
    shift = lists_ref[0, a, 1, k, r]
    return owner, HR + shift * rows + lists_ref[0, a, 2, k, r], shift == 0


def serve(lists_ref, number_ref, send_ref, a, d, early, rows, per_row):
    me = lax.axis_index("lon")
    base = d * STRIDE
    near = jnp.int32(0)
    other = jnp.int32(0)
    for r in range(rows):
        for k in range(per_row):
            owner, row, own_band = decode(lists_ref, number_ref, r, a, k, rows)
            hit = owner == me
            ahead = hit & own_band & (near < early)
            slot = jnp.where(ahead, near, early + other)
            send_ref[base + jnp.where(hit, slot, TRASH)] = row
            near = near + jnp.where(ahead, 1, 0)
            other = other + jnp.where(hit, 1, 0) - jnp.where(ahead, 1, 0)
    send_ref[base + COUNT] = other


def prepare_kernel(tiles, bands, per_row, lists_ref, number_ref, fields_ref, *rest):
    rows_ref, send_ref, *rest = rest
    edges = rest[: 1 if bands == 2 else 2]
    held, wide, sems = rest[len(edges) :]
    rows, channels, _ = rows_ref.shape
    me = lax.axis_index("lon")
    dump = rows + 2 * HR
    chunk = 16
    copies = []
    for i, c in enumerate(range(0, channels, chunk)):
        span = pl.ds(c * rows, chunk * rows)
        copies.append(pltpu.make_async_copy(fields_ref.at[span], held.at[span], sems.at[i]))
        copies[-1].start()
    for d in range(1, tiles):
        for s in range(sum(regions(d, tiles))):
            send_ref[d * STRIDE + s] = dump
    if tiles <= 4:
        for d in range(1, tiles):
            early = regions(d, tiles)[0]
            serve(lists_ref, number_ref, send_ref, wrap(me + d - tiles, tiles), d, early, rows, per_row)
    else:

        @pl.loop(1, tiles)
        def _(d):
            early = jnp.where(d == tiles // 2, EARLY, 0)
            serve(lists_ref, number_ref, send_ref, wrap(me + d - tiles, tiles), d, early, rows, per_row)

    for i, c in enumerate(range(0, channels, chunk)):
        copies[i].wait()
        span = slice(c * rows, (c + chunk) * rows)
        wide[span] = held[span].astype(F32)
        for r in range(rows):
            rows_ref[r, c : c + chunk] = wide[pl.ds(c * rows + r, chunk, stride=rows), :].astype(BF16)
    if bands == 2:
        start = jnp.where(lax.axis_index("lat") == 0, rows - HR, 0)
        edges[0][...] = rows_ref[pl.ds(start, HR)]
    else:
        edges[0][...] = rows_ref[0:HR]
        edges[1][...] = rows_ref[rows - HR : rows]


def pack_kernel(tiles, send_ref, rows_ref, before_ref, after_ref, ext_ref, *rest):
    base, spare = rest[: tiles - 1], rest[tiles - 1 :]
    rows = rows_ref.shape[0]
    ext_ref[0:HR] = before_ref[...]
    ext_ref[HR : HR + rows] = rows_ref[...]
    ext_ref[HR + rows : HR + rows + HR] = after_ref[...]
    for d in range(1, tiles):
        for s in range(EVEN):
            base[d - 1][s] = ext_ref[send_ref[d * STRIDE + s]]
    for d in range(1, tiles):
        _, shared, more = regions(d, tiles)

        @pl.when(send_ref[d * STRIDE + COUNT] > shared)
        def _():
            for s in range(more):
                spare[d - 1][s] = ext_ref[send_ref[d * STRIDE + EVEN + s]]


def arrival_kernel(tiles, per_row, lists_ref, number_ref, cot_ref, taps_ref, *rest):
    cot_rows_ref, mix_ref, place_ref, own_ref, wide, near, other = rest
    rows, channels, cols = cot_rows_ref.shape
    me = lax.axis_index("lon")
    entries = rows * per_row
    ext = rows + 2 * HR
    for s in range(CAP):
        own_ref[s] = ext
    serve(lists_ref, number_ref, own_ref, me, 0, 0, rows, per_row)
    for d in range(tiles + 1):
        near[d] = 0
        other[d] = 0

    def place(r):
        for k in range(per_row):
            owner, ext_row, own_band = decode(lists_ref, number_ref, r, me, k, rows)
            used = owner >= 0
            d = jnp.where(used, wrap(me - owner, tiles), tiles)
            early = jnp.where((d == tiles // 2) & (d > 0), EARLY, 0)
            ahead = own_band & (near[d] < early)
            slot = d * PLACES + jnp.where(ahead, near[d], early + other[d])
            source = jnp.where(owner == me, tiles * PLACES + ext_row, slot)
            place_ref[r * per_row + k] = jnp.where(used, source, tiles * PLACES + ext)
            place_ref[entries + r * per_row + k] = jnp.where(used, slot, tiles * PLACES)
            near[d] = near[d] + jnp.where(ahead, 1, 0)
            other[d] = other[d] + jnp.where(ahead, 0, 1)

    pl.loop(0, rows)(place)
    for d in range(tiles):
        place_ref[2 * entries + d] = other[d]

    wide[...] = cot_ref[...].astype(F32)
    for r in range(rows):
        cot_rows_ref[r] = wide[pl.ds(r, channels, stride=rows), :].astype(BF16)
    w0, w1, w2, w3 = (taps_ref[j] for j in range(4))
    cell = lax.broadcasted_iota(jnp.int32, w0.shape, 1)
    first, last, late = cell == 0, cell == cols - 1, cell == cols - 2
    mix_ref[0] = pltpu.roll(jnp.where(first, 0.0, w0), cols - 1, 1)
    mix_ref[1] = w1 + jnp.where(first, w0, 0.0) + jnp.where(last, w2 + w3, 0.0)
    mix_ref[2] = pltpu.roll(jnp.where(last, 0.0, w2) + jnp.where(late, w3, 0.0), 1, 1)
    mix_ref[3] = pltpu.roll(jnp.where(last | late, 0.0, w3), 2, 1)


def compute_kernel(tiles, per_row, place_ref, mix_ref, cot_ref, ext_ref, *rest):
    n = tiles - 1
    base, spare, rest = rest[:n], rest[n : 2 * n], rest[2 * n :]
    own_out, early_out, rest = rest[0], rest[1], rest[2:]
    shared_out, spare_out, (grad_ref, blocks, terms) = rest[:n], rest[n : 2 * n], rest[2 * n :]
    rows, channels, cols = cot_ref.shape
    entries = rows * per_row
    ext = rows + 2 * HR
    part = min(channels, 32)
    blocks[tiles * PLACES : tiles * PLACES + ext] = ext_ref[0:ext]
    blocks[tiles * PLACES + ext] = jnp.zeros((channels, cols), BF16)
    for d in range(1, tiles):
        _, shared, more = regions(d, tiles)
        at = d * PLACES
        blocks[at : at + EVEN] = base[d - 1][...]

        @pl.when(place_ref[2 * entries + d] > shared)
        def _():
            blocks[at + EVEN : at + EVEN + more] = spare[d - 1][...]

    def row(r, _):
        source = [place_ref[r * per_row + k] for k in range(per_row)]
        target = [place_ref[entries + r * per_row + k] for k in range(per_row)]
        mix = [[mix_ref[j, pl.ds(r * per_row + k, 1), :] for j in range(4)] for k in range(per_row)]
        for lo in range(0, channels, part):
            block = [blocks[source[k], lo : lo + part].astype(F32) for k in range(per_row)]
            tap = [sum(block[k] * mix[k][j] for k in range(per_row)) for j in range(4)]
            interp = (tap[1] + pltpu.roll(tap[0], 1, 1)) + (
                pltpu.roll(tap[2], cols - 1, 1) + pltpu.roll(tap[3], cols - 2, 1)
            )
            bent = jnp.tanh(interp)
            scaled = cot_ref[r, lo : lo + part].astype(F32) * (2.0 - bent * bent)
            scaled = scaled.astype(BF16).astype(F32)
            moved = [
                pltpu.roll(scaled, cols - 1, 1),
                scaled,
                pltpu.roll(scaled, 1, 1),
                pltpu.roll(scaled, 2, 1),
            ]
            for k in range(per_row):
                term = (moved[0] * mix[k][0] + moved[1] * mix[k][1]) + (
                    moved[2] * mix[k][2] + moved[3] * mix[k][3]
                )
                terms[target[k], lo : lo + part] = term.astype(BF16)
                for j in range(4):
                    at = (r * per_row + k) * 4 + j
                    product = jnp.sum((block[k] * moved[j]).reshape(part // 8, 8, cols), axis=0)
                    grad_ref[at] = product if lo == 0 else grad_ref[at] + product
        return 0

    lax.fori_loop(0, rows, row, 0, unroll=4)
    for d in range(1, tiles):
        early, shared, more = regions(d, tiles)
        at = d * PLACES
        shared_out[d - 1][...] = terms[at + early : at + EVEN]
        if early:
            early_out[...] = terms[at : at + early]

        @pl.when(place_ref[2 * entries + d] > shared)
        def _():
            spare_out[d - 1][...] = terms[at + EVEN : at + EVEN + more]

    own_out[...] = terms[0:CAP]


def gradient_kernel(partial_ref, out_ref):
    sums = jnp.sum(partial_ref[...], axis=1)
    count, cols = sums.shape
    tap = lax.broadcasted_iota(jnp.int32, sums.shape, 0) & 3
    cell = lax.broadcasted_iota(jnp.int32, sums.shape, 1)
    grads = jnp.where(tap == 0, pltpu.roll(sums, 1, 1), sums)
    grads = jnp.where(tap == 2, pltpu.roll(sums, cols - 1, 1), grads)
    grads = jnp.where(tap == 3, pltpu.roll(sums, cols - 2, 1), grads)
    following = pltpu.roll(grads, count - 1, 0)
    previous = pltpu.roll(grads, 1, 0)
    second = pltpu.roll(grads, 2, 0)
    fixed = jnp.where((tap == 0) & (cell == 0), following, grads)
    fixed = jnp.where((tap == 2) & (cell == cols - 1), previous, fixed)
    fixed = jnp.where((tap == 3) & (cell == cols - 2), previous, fixed)
    fixed = jnp.where((tap == 3) & (cell == cols - 1), second, fixed)
    out_ref[...] = fixed.astype(BF16)


def add_own_kernel(table_ref, own_ref, total_ref):
    total_ref[...] = jnp.zeros_like(total_ref)
    for s in range(CAP):
        at = table_ref[s]
        total_ref[at] = total_ref[at] + own_ref[s].astype(F32)


def add_shared_kernel(tiles, bands, send_ref, _, *rest):
    shared, spare, (total_ref, *edges) = rest[: tiles - 1], rest[tiles - 1 : 2 * tiles - 2], rest[2 * tiles - 2 :]
    ext = total_ref.shape[0] - 1
    for d in range(1, tiles):
        early, count, more = regions(d, tiles)
        for s in range(count):
            at = send_ref[d * STRIDE + early + s]
            total_ref[at] = total_ref[at] + shared[d - 1][s].astype(F32)

        @pl.when(send_ref[d * STRIDE + COUNT] > count)
        def _():
            for s in range(more):
                at = send_ref[d * STRIDE + EVEN + s]
                total_ref[at] = total_ref[at] + spare[d - 1][s].astype(F32)

    if bands == 2:
        start = jnp.where(lax.axis_index("lat") == 0, ext - HR, 0)
        edges[0][...] = total_ref[pl.ds(start, HR)].astype(BF16)
    else:
        edges[0][...] = total_ref[0:HR].astype(BF16)
        edges[1][...] = total_ref[ext - HR : ext].astype(BF16)


def finish_kernel(tiles, bands, rows, send_ref, _, early_ref, above_ref, below_ref, out_ref, total_ref):
    channels = total_ref.shape[1]
    d = tiles // 2
    for s in range(EARLY):
        at = send_ref[d * STRIDE + s]
        total_ref[at] = total_ref[at] + early_ref[s].astype(F32)
    band = lax.axis_index("lat")
    for r in range(rows):
        value = total_ref[HR + r]
        if r < HR:
            value = value + jnp.where(band > 0, above_ref[r].astype(F32), 0.0)
        if r >= rows - HR:
            value = value + jnp.where(band < bands - 1, below_ref[r - rows + HR].astype(F32), 0.0)
        out_ref[pl.ds(r, channels, stride=rows), :] = value


def swap_lat(edges, bands):
    if bands == 2:
        got = lax.ppermute(edges[0], "lat", [(0, 1), (1, 0)])
        return got, got
    down = [(i, i + 1) for i in range(bands - 1)]
    up = [(i + 1, i) for i in range(bands - 1)]
    return lax.ppermute(edges[1], "lat", down), lax.ppermute(edges[0], "lat", up)


def local(fields, arrival_cot, weights, departures, counts):
    lev_dev, field_count, rows, cols = fields.shape
    channels = lev_dev * field_count
    tiles = lax.axis_size("lon")
    bands = lax.axis_size("lat")
    per_row, taps = weights.shape[3], weights.shape[4]
    entries = rows * per_row
    ext = rows + 2 * HR
    partners = tiles - 1
    middle = tiles // 2
    params = pltpu.CompilerParams(vmem_limit_bytes=48 * 1024 * 1024)

    def call(kernel, out_shape, in_specs, out_specs, scratch=(), name=None, aliases={}):
        return pl.pallas_call(
            kernel,
            out_shape=out_shape,
            in_specs=in_specs,
            out_specs=out_specs,
            scratch_shapes=list(scratch),
            compiler_params=params,
            input_output_aliases=aliases,
            name=name,
        )

    def array(*shape, dtype=BF16):
        return jax.ShapeDtypeStruct(shape, dtype)

    def move(part, d):
        return lax.ppermute(part, "lon", [(i, (i + d) % tiles) for i in range(tiles)])

    def move_all(parts, sign):
        out = [None] * partners
        for d in [middle] + [d for d in range(1, tiles) if d != middle]:
            out[d - 1] = move(parts[d - 1], sign * d)
        return out

    def move_spare(needed, parts, sign):
        return lax.cond(needed, lambda parts: move_all(parts, sign), lambda parts: parts, list(parts))

    lists = jnp.transpose(departures, (0, 2, 4, 3, 1))
    number = jnp.transpose(counts, (0, 2, 1))

    edge = (array(HR, channels, cols),) * (1 if bands == 2 else 2)
    base_slots = (array(EVEN, channels, cols),) * partners
    shared_slots = tuple(array(regions(d, tiles)[1], channels, cols) for d in range(1, tiles))
    spare_slots = tuple(array(regions(d, tiles)[2], channels, cols) for d in range(1, tiles))

    row_blocks, send_rows, *edges = call(
        functools.partial(prepare_kernel, tiles, bands, per_row),
        (array(rows, channels, cols), array(tiles * STRIDE, dtype=jnp.int32)) + edge,
        [whole(SMEM), whole(SMEM), whole(pl.ANY)],
        (whole(VMEM), whole(SMEM)) + (whole(VMEM),) * len(edge),
        [
            VMEM((channels * rows, cols), BF16),
            VMEM((channels * rows, cols), F32),
            pltpu.SemaphoreType.DMA((channels // 16,)),
        ],
        "prepare",
    )(lists, number, fields.reshape(channels * rows, cols))
    before, after = swap_lat(edges, bands)

    ext_blocks, *rest = call(
        functools.partial(pack_kernel, tiles),
        (array(ext + 1, channels, cols),) + base_slots + spare_slots,
        [whole(SMEM)] + [whole(VMEM)] * 3,
        (whole(VMEM),) * (1 + 2 * partners),
        (),
        "pack",
    )(send_rows, row_blocks, before, after)
    base = move_all(rest[:partners], 1)

    tile = jnp.arange(tiles, dtype=jnp.int32)
    entry = jnp.arange(per_row, dtype=jnp.int32)
    named = (entry[:, None] < number[0][:, None, :]) & (lists[0, :, 0] == tile[:, None, None, None])
    own_band = lists[0, :, 1] == 0
    near = jnp.sum(jnp.where(named & own_band, 1, 0), axis=(2, 3))
    far = jnp.sum(jnp.where(named & ~own_band, 1, 0), axis=(2, 3))
    distance = (tile[None, :] - tile[:, None]) % tiles
    early = jnp.where(distance == middle, EARLY, 0)
    needed = jnp.any((far + jnp.maximum(near - early, 0) > EVEN - early) & (distance > 0))
    spare = move_spare(needed, rest[partners:], 1)

    mixing = weights.reshape(rows, per_row, taps, cols).astype(F32)
    mixing = jnp.transpose(mixing, (2, 0, 1, 3)).reshape(taps, entries, cols)
    cot_rows, mix, places, own_table = call(
        functools.partial(arrival_kernel, tiles, per_row),
        (
            array(rows, channels, cols),
            array(taps, entries, cols, dtype=F32),
            array(2 * entries + tiles, dtype=jnp.int32),
            array(STRIDE, dtype=jnp.int32),
        ),
        [whole(SMEM), whole(SMEM), whole(VMEM), whole(VMEM)],
        (whole(VMEM), whole(VMEM), whole(SMEM), whole(SMEM)),
        [VMEM((channels * rows, cols), F32)] + [SMEM((tiles + 1,), jnp.int32)] * 2,
        "arrival",
    )(lists, number, arrival_cot.reshape(channels * rows, cols), mixing)

    own, early, *rest = call(
        functools.partial(compute_kernel, tiles, per_row),
        (array(CAP, channels, cols), array(EARLY, channels, cols))
        + shared_slots
        + spare_slots
        + (array(entries * taps, 8, cols, dtype=F32),),
        [whole(SMEM)] + [whole(VMEM)] * (3 + 2 * partners),
        (whole(VMEM),) * (3 + 2 * partners),
        [
            VMEM((tiles * PLACES + ext + 1, channels, cols), BF16),
            VMEM((tiles * PLACES + 1, channels, cols), BF16),
        ],
        "compute",
    )(places, mix, cot_rows, ext_blocks, *base, *spare)
    grads = rest[-1]
    shared = move_all(rest[:partners], -1)
    early = move(early, -middle)
    spare = move_spare(needed, rest[partners : 2 * partners], -1)

    sums = array(ext + 1, channels, cols, dtype=F32)
    total = call(add_own_kernel, sums, [whole(SMEM), whole(VMEM)], whole(VMEM), (), "add_own")(
        own_table, own
    )
    total, *edges = call(
        functools.partial(add_shared_kernel, tiles, bands),
        (sums,) + edge,
        [whole(SMEM)] + [whole(VMEM)] * (1 + 2 * partners),
        (whole(VMEM),) * (1 + len(edge)),
        (),
        "add_shared",
        {1: 0},
    )(send_rows, total, *shared, *spare)
    from_above, from_below = swap_lat(edges, bands)
    source, _ = call(
        functools.partial(finish_kernel, tiles, bands, rows),
        (array(channels * rows, cols, dtype=F32), sums),
        [whole(SMEM)] + [whole(VMEM)] * 4,
        (whole(VMEM),) * 2,
        (),
        "finish",
        {1: 1},
    )(send_rows, total, early, from_above, from_below)

    grads, _ = lax.optimization_barrier((grads, edges[0]))
    weight_grad = call(
        gradient_kernel,
        array(entries * taps, cols),
        [whole(VMEM)],
        whole(VMEM),
        (),
        "gradient",
    )(grads)
    return source.reshape(fields.shape), weight_grad.reshape(weights.shape)


def solution(mesh):
    return jax.shard_map(
        local,
        mesh=mesh,
        in_specs=(
            P("lev", "ens", "lat", "lon"),
            P("lev", "ens", "lat", "lon"),
            P("lev", "lat", "lon", "ens", None, None),
            P("lev", "lat", None, "ens", None),
            P("lev", "lat", "ens"),
        ),
        out_specs=(P("lev", "ens", "lat", "lon"), P("lev", "lat", "lon", "ens", None, None)),
        check_vma=False,
    )
```

```python
import functools

import jax
import jax.numpy as jnp
from jax import lax
from jax.experimental import pallas as pl
from jax.experimental.pallas import tpu as pltpu
from jax.sharding import PartitionSpec as P

HR = 2
CAP = 11
BASE = 8
SPARE = CAP - BASE
PARTS = 2
STRIDE = 16
TRASH = STRIDE - 2
COUNT = STRIDE - 1
BF16 = jnp.bfloat16
F32 = jnp.float32
VMEM = pltpu.VMEM
SMEM = pltpu.SMEM


def whole(space):
    return pl.BlockSpec(memory_space=space)


def wrap(value, size):
    return jnp.where(value < 0, value + size, value)


def decode(lists_ref, number_ref, r, a, k, rows):
    used = k < number_ref[0, a, r]
    owner = jnp.where(used, lists_ref[0, a, 0, k, r], -1)
    return owner, HR + lists_ref[0, a, 1, k, r] * rows + lists_ref[0, a, 2, k, r]


def serve(lists_ref, number_ref, send_ref, a, d, rows, per_row):
    me = lax.axis_index("lon")
    base = d * STRIDE
    filled = jnp.int32(0)
    for r in range(rows):
        for k in range(per_row):
            owner, row = decode(lists_ref, number_ref, r, a, k, rows)
            send_ref[base + jnp.where(owner == me, filled, TRASH)] = row
            filled = filled + jnp.where(owner == me, 1, 0)
    send_ref[base + COUNT] = filled


def prepare_kernel(tiles, bands, per_row, lists_hbm, number_hbm, fields_hbm, *rest):
    rows_ref, send_ref, *rest = rest
    edges = rest[: 1 if bands == 2 else 2]
    lists_ref, number_ref, held, wide, list_sem, number_sem, sems = rest[len(edges) :]
    rows, channels, _ = rows_ref.shape
    me = lax.axis_index("lon")
    dump = rows + 2 * HR
    chunk = 16
    lists_copy = pltpu.make_async_copy(lists_hbm, lists_ref, list_sem)
    number_copy = pltpu.make_async_copy(number_hbm, number_ref, number_sem)
    lists_copy.start()
    number_copy.start()
    copies = []
    for i, c in enumerate(range(0, channels, chunk)):
        span = pl.ds(c * rows, chunk * rows)
        copies.append(pltpu.make_async_copy(fields_hbm.at[span], held.at[span], sems.at[i]))
        copies[-1].start()
    for d in range(1, tiles):
        for s in range(CAP):
            send_ref[d * STRIDE + s] = dump
    lists_copy.wait()
    number_copy.wait()
    if tiles <= 4:
        for d in range(1, tiles):
            serve(lists_ref, number_ref, send_ref, wrap(me + d - tiles, tiles), d, rows, per_row)
    else:

        @pl.loop(1, tiles)
        def _(d):
            serve(lists_ref, number_ref, send_ref, wrap(me + d - tiles, tiles), d, rows, per_row)

    for i, c in enumerate(range(0, channels, chunk)):
        copies[i].wait()
        span = slice(c * rows, (c + chunk) * rows)
        wide[span] = held[span].astype(F32)
        for r in range(rows):
            rows_ref[r, c : c + chunk] = wide[pl.ds(c * rows + r, chunk, stride=rows), :].astype(BF16)
    if bands == 2:
        start = jnp.where(lax.axis_index("lat") == 0, rows - HR, 0)
        edges[0][...] = rows_ref[pl.ds(start, HR)]
    else:
        edges[0][...] = rows_ref[0:HR]
        edges[1][...] = rows_ref[rows - HR : rows]


def pack_kernel(tiles, start, send_ref, rows_ref, before_ref, after_ref, ext_ref, *rest):
    base, spare = rest[: tiles - 1], rest[tiles - 1 :]
    rows = rows_ref.shape[0]
    part = slice(start, start + ext_ref.shape[1])
    ext_ref[0:HR] = before_ref[:, part]
    ext_ref[HR : HR + rows] = rows_ref[:, part]
    ext_ref[HR + rows : HR + rows + HR] = after_ref[:, part]
    for d in range(1, tiles):
        for s in range(BASE):
            base[d - 1][s] = ext_ref[send_ref[d * STRIDE + s]]
    for d in range(1, tiles):

        @pl.when(send_ref[d * STRIDE + COUNT] > BASE)
        def _():
            for s in range(SPARE):
                spare[d - 1][s] = ext_ref[send_ref[d * STRIDE + BASE + s]]


def arrival_kernel(tiles, per_row, lists_ref, number_ref, cot_ref, taps_ref, *rest):
    cot_rows_ref, mix_ref, place_ref, own_ref, wide, taken = rest
    rows, channels, cols = cot_rows_ref.shape
    me = lax.axis_index("lon")
    entries = rows * per_row
    ext = rows + 2 * HR
    for s in range(CAP):
        own_ref[s] = ext
    serve(lists_ref, number_ref, own_ref, me, 0, rows, per_row)
    for d in range(tiles + 1):
        taken[d] = 0

    def place(r):
        for k in range(per_row):
            owner, ext_row = decode(lists_ref, number_ref, r, me, k, rows)
            used = owner >= 0
            d = jnp.where(used, wrap(me - owner, tiles), tiles)
            slot = d * STRIDE + taken[d]
            source = jnp.where(owner == me, tiles * STRIDE + ext_row, slot)
            place_ref[r * per_row + k] = jnp.where(used, source, tiles * STRIDE + ext)
            place_ref[entries + r * per_row + k] = jnp.where(used, slot, tiles * STRIDE)
            taken[d] = taken[d] + 1

    pl.loop(0, rows)(place)
    for d in range(tiles):
        place_ref[2 * entries + d] = taken[d]

    wide[...] = cot_ref[...].astype(F32)
    for r in range(rows):
        cot_rows_ref[r] = wide[pl.ds(r, channels, stride=rows), :].astype(BF16)
    w0, w1, w2, w3 = (taps_ref[j] for j in range(4))
    cell = lax.broadcasted_iota(jnp.int32, w0.shape, 1)
    first, last, late = cell == 0, cell == cols - 1, cell == cols - 2
    mix_ref[0] = pltpu.roll(jnp.where(first, 0.0, w0), cols - 1, 1)
    mix_ref[1] = w1 + jnp.where(first, w0, 0.0) + jnp.where(last, w2 + w3, 0.0)
    mix_ref[2] = pltpu.roll(jnp.where(last, 0.0, w2) + jnp.where(late, w3, 0.0), 1, 1)
    mix_ref[3] = pltpu.roll(jnp.where(last | late, 0.0, w3), 2, 1)


def compute_kernel(tiles, per_row, start, place_ref, mix_ref, cot_ref, ext_ref, *rest):
    n = tiles - 1
    base, spare, rest = rest[:n], rest[n : 2 * n], rest[2 * n :]
    own_out, base_out, spare_out, rest = rest[0], rest[1 : n + 1], rest[n + 1 : 2 * n + 1], rest[2 * n + 1 :]
    grad_ref, blocks, terms = rest
    rows, _, cols = cot_ref.shape
    channels = ext_ref.shape[1]
    entries = rows * per_row
    ext = rows + 2 * HR
    part = min(channels, 32)
    blocks[tiles * STRIDE : tiles * STRIDE + ext] = ext_ref[0:ext]
    blocks[tiles * STRIDE + ext] = jnp.zeros((channels, cols), BF16)
    for d in range(1, tiles):
        at = d * STRIDE
        blocks[at : at + BASE] = base[d - 1][...]

        @pl.when(place_ref[2 * entries + d] > BASE)
        def _():
            blocks[at + BASE : at + CAP] = spare[d - 1][...]

    def row(r, _):
        source = [place_ref[r * per_row + k] for k in range(per_row)]
        target = [place_ref[entries + r * per_row + k] for k in range(per_row)]
        mix = [[mix_ref[j, pl.ds(r * per_row + k, 1), :] for j in range(4)] for k in range(per_row)]
        for lo in range(0, channels, part):
            block = [blocks[source[k], lo : lo + part].astype(F32) for k in range(per_row)]
            tap = [sum(block[k] * mix[k][j] for k in range(per_row)) for j in range(4)]
            interp = (tap[1] + pltpu.roll(tap[0], 1, 1)) + (
                pltpu.roll(tap[2], cols - 1, 1) + pltpu.roll(tap[3], cols - 2, 1)
            )
            bent = jnp.tanh(interp)
            scaled = cot_ref[r, start + lo : start + lo + part].astype(F32) * (2.0 - bent * bent)
            scaled = scaled.astype(BF16).astype(F32)
            moved = [
                pltpu.roll(scaled, cols - 1, 1),
                scaled,
                pltpu.roll(scaled, 1, 1),
                pltpu.roll(scaled, 2, 1),
            ]
            for k in range(per_row):
                term = (moved[0] * mix[k][0] + moved[1] * mix[k][1]) + (
                    moved[2] * mix[k][2] + moved[3] * mix[k][3]
                )
                terms[target[k], lo : lo + part] = term.astype(BF16)
                for j in range(4):
                    at = (r * per_row + k) * 4 + j
                    product = jnp.sum((block[k] * moved[j]).reshape(part // 8, 8, cols), axis=0)
                    grad_ref[at] = product if lo == 0 else grad_ref[at] + product
        return 0

    lax.fori_loop(0, rows, row, 0, unroll=4)
    for d in range(1, tiles):
        at = d * STRIDE
        base_out[d - 1][...] = terms[at : at + BASE]

        @pl.when(place_ref[2 * entries + d] > BASE)
        def _():
            spare_out[d - 1][...] = terms[at + BASE : at + CAP]

    own_out[...] = terms[0:CAP]


def gradient_kernel(*refs):
    *partial_refs, out_ref = refs
    sums = jnp.sum(sum(ref[...] for ref in partial_refs), axis=1)
    count, cols = sums.shape
    tap = lax.broadcasted_iota(jnp.int32, sums.shape, 0) & 3
    cell = lax.broadcasted_iota(jnp.int32, sums.shape, 1)
    grads = jnp.where(tap == 0, pltpu.roll(sums, 1, 1), sums)
    grads = jnp.where(tap == 2, pltpu.roll(sums, cols - 1, 1), grads)
    grads = jnp.where(tap == 3, pltpu.roll(sums, cols - 2, 1), grads)
    following = pltpu.roll(grads, count - 1, 0)
    previous = pltpu.roll(grads, 1, 0)
    second = pltpu.roll(grads, 2, 0)
    fixed = jnp.where((tap == 0) & (cell == 0), following, grads)
    fixed = jnp.where((tap == 2) & (cell == cols - 1), previous, fixed)
    fixed = jnp.where((tap == 3) & (cell == cols - 2), previous, fixed)
    fixed = jnp.where((tap == 3) & (cell == cols - 1), second, fixed)
    out_ref[...] = fixed.astype(BF16)


def add_own_kernel(table_ref, own_ref, total_ref):
    total_ref[...] = jnp.zeros_like(total_ref)
    for s in range(CAP):
        at = table_ref[s]
        total_ref[at] = total_ref[at] + own_ref[s].astype(F32)


def add_kernel(tiles, bands, send_ref, _, *rest):
    n = tiles - 1
    base, spare, (total_ref, *edges) = rest[:n], rest[n : 2 * n], rest[2 * n :]
    ext = total_ref.shape[0] - 1
    for d in range(1, tiles):
        for s in range(BASE):
            at = send_ref[d * STRIDE + s]
            total_ref[at] = total_ref[at] + base[d - 1][s].astype(F32)

        @pl.when(send_ref[d * STRIDE + COUNT] > BASE)
        def _():
            for s in range(SPARE):
                at = send_ref[d * STRIDE + BASE + s]
                total_ref[at] = total_ref[at] + spare[d - 1][s].astype(F32)

    if bands == 2:
        start = jnp.where(lax.axis_index("lat") == 0, ext - HR, 0)
        edges[0][...] = total_ref[pl.ds(start, HR)].astype(BF16)
    else:
        edges[0][...] = total_ref[0:HR].astype(BF16)
        edges[1][...] = total_ref[ext - HR : ext].astype(BF16)


def finish_kernel(bands, rows, start, total_ref, above_ref, below_ref, *rest):
    out_hbm, held, sems = rest[-3:]
    channels = total_ref.shape[1]
    band = lax.axis_index("lat")
    chunk = 16
    copies = []
    for i, c in enumerate(range(0, channels, chunk)):
        part = slice(c, c + chunk)
        for r in range(rows):
            value = total_ref[HR + r, part]
            if r < HR:
                value = value + jnp.where(band > 0, above_ref[r, part].astype(F32), 0.0)
            if r >= rows - HR:
                below = below_ref[r - rows + HR, part].astype(F32)
                value = value + jnp.where(band < bands - 1, below, 0.0)
            held[pl.ds(c * rows + r, chunk, stride=rows), :] = value
        source = held.at[pl.ds(c * rows, chunk * rows)]
        target = out_hbm.at[pl.ds((start + c) * rows, chunk * rows)]
        copies.append(pltpu.make_async_copy(source, target, sems.at[i]))
        copies[-1].start()
    for copy in copies:
        copy.wait()


def swap_lat(edges, bands):
    if bands == 2:
        got = lax.ppermute(edges[0], "lat", [(0, 1), (1, 0)])
        return got, got
    down = [(i, i + 1) for i in range(bands - 1)]
    up = [(i + 1, i) for i in range(bands - 1)]
    return lax.ppermute(edges[1], "lat", down), lax.ppermute(edges[0], "lat", up)


def local(fields, arrival_cot, weights, departures, counts):
    lev_dev, field_count, rows, cols = fields.shape
    channels = lev_dev * field_count
    tiles = lax.axis_size("lon")
    bands = lax.axis_size("lat")
    per_row, taps = weights.shape[3], weights.shape[4]
    entries = rows * per_row
    ext = rows + 2 * HR
    partners = tiles - 1
    middle = tiles // 2
    width = channels // PARTS
    params = pltpu.CompilerParams(vmem_limit_bytes=48 * 1024 * 1024)

    def call(kernel, out_shape, in_specs, out_specs, scratch=(), name=None, aliases={}):
        return pl.pallas_call(
            kernel,
            out_shape=out_shape,
            in_specs=in_specs,
            out_specs=out_specs,
            scratch_shapes=list(scratch),
            compiler_params=params,
            input_output_aliases=aliases,
            name=name,
        )

    def array(*shape, dtype=BF16):
        return jax.ShapeDtypeStruct(shape, dtype)

    def move(part, d):
        return lax.ppermute(part, "lon", [(i, (i + d) % tiles) for i in range(tiles)])

    def move_all(parts, sign):
        out = [None] * partners
        for d in [middle] + [d for d in range(1, tiles) if d != middle]:
            out[d - 1] = move(parts[d - 1], sign * d)
        return out

    def move_spare(parts, sign):
        return lax.cond(needed, lambda parts: move_all(parts, sign), lambda parts: parts, list(parts))

    lists = jnp.transpose(departures, (0, 2, 4, 3, 1))
    number = jnp.transpose(counts, (0, 2, 1))

    edge_count = 1 if bands == 2 else 2
    edge = (array(HR, channels, cols),) * edge_count
    half_edge = (array(HR, width, cols),) * edge_count
    base_slots = (array(BASE, width, cols),) * partners
    spare_slots = (array(SPARE, width, cols),) * partners

    def hbm(value):
        return pltpu.with_memory_space_constraint(value, pltpu.HBM)

    row_blocks, send_rows, *edges = call(
        functools.partial(prepare_kernel, tiles, bands, per_row),
        (array(rows, channels, cols), array(tiles * STRIDE, dtype=jnp.int32)) + edge,
        [whole(pltpu.HBM)] * 3,
        (whole(VMEM), whole(SMEM)) + (whole(VMEM),) * edge_count,
        [
            SMEM(lists.shape, jnp.int32),
            SMEM(number.shape, jnp.int32),
            VMEM((channels * rows, cols), BF16),
            VMEM((channels * rows, cols), F32),
            pltpu.SemaphoreType.DMA,
            pltpu.SemaphoreType.DMA,
            pltpu.SemaphoreType.DMA((channels // 16,)),
        ],
        "prepare",
    )(hbm(lists), hbm(number), hbm(fields.reshape(channels * rows, cols)))
    before, after = swap_lat(edges, bands)

    tile = jnp.arange(tiles, dtype=jnp.int32)
    entry = jnp.arange(per_row, dtype=jnp.int32)
    named = (entry[:, None] < number[0][:, None, :]) & (lists[0, :, 0] == tile[:, None, None, None])
    filled = jnp.sum(jnp.where(named, 1, 0), axis=(2, 3))
    needed = jnp.any((filled > BASE) & (tile[None, :] != tile[:, None]))

    mixing = weights.reshape(rows, per_row, taps, cols).astype(F32)
    mixing = jnp.transpose(mixing, (2, 0, 1, 3)).reshape(taps, entries, cols)

    sent = []
    for start in range(0, channels, width):
        ext_blocks, *slots = call(
            functools.partial(pack_kernel, tiles, start),
            (array(ext + 1, width, cols),) + base_slots + spare_slots,
            [whole(SMEM)] + [whole(VMEM)] * 3,
            (whole(VMEM),) * (1 + 2 * partners),
            (),
            "pack",
        )(send_rows, row_blocks, before, after)
        sent.append((ext_blocks, move_all(slots[:partners], 1), move_spare(slots[partners:], 1)))

    cot_rows, mix, places, own_table = call(
        functools.partial(arrival_kernel, tiles, per_row),
        (
            array(rows, channels, cols),
            array(taps, entries, cols, dtype=F32),
            array(2 * entries + tiles, dtype=jnp.int32),
            array(STRIDE, dtype=jnp.int32),
        ),
        [whole(SMEM), whole(SMEM), whole(VMEM), whole(VMEM)],
        (whole(VMEM), whole(VMEM), whole(SMEM), whole(SMEM)),
        [VMEM((channels * rows, cols), F32), SMEM((tiles + 1,), jnp.int32)],
        "arrival",
    )(lists, number, arrival_cot.reshape(channels * rows, cols), mixing)

    back, partial = [], []
    for i, (ext_blocks, base, spare) in enumerate(sent):
        own, *slots = call(
            functools.partial(compute_kernel, tiles, per_row, i * width),
            (array(CAP, width, cols),)
            + base_slots
            + spare_slots
            + (array(entries * taps, 8, cols, dtype=F32),),
            [whole(SMEM)] + [whole(VMEM)] * (3 + 2 * partners),
            (whole(VMEM),) * (2 + 2 * partners),
            [
                VMEM((tiles * STRIDE + ext + 1, width, cols), BF16),
                VMEM((tiles * STRIDE + 1, width, cols), BF16),
            ],
            "compute",
        )(places, mix, cot_rows, ext_blocks, *base, *spare)
        back.append((own, move_all(slots[:partners], -1), move_spare(slots[partners : 2 * partners], -1)))
        partial.append(slots[-1])

    sums = array(ext + 1, width, cols, dtype=F32)
    source = None
    for i, (own, base, spare) in enumerate(back):
        total = call(add_own_kernel, sums, [whole(SMEM), whole(VMEM)], whole(VMEM), (), "add_own")(
            own_table, own
        )
        total, *edges = call(
            functools.partial(add_kernel, tiles, bands),
            (sums,) + half_edge,
            [whole(SMEM)] + [whole(VMEM)] * (1 + 2 * partners),
            (whole(VMEM),) * (1 + edge_count),
            (),
            "add",
            {1: 0},
        )(send_rows, total, *base, *spare)
        from_above, from_below = swap_lat(edges, bands)
        earlier = [] if source is None else [source]
        source = call(
            functools.partial(finish_kernel, bands, rows, i * width),
            array(channels * rows, cols, dtype=F32),
            [whole(VMEM)] * 3 + [whole(pltpu.HBM)] * len(earlier),
            whole(pltpu.HBM),
            [VMEM((width * rows, cols), F32), pltpu.SemaphoreType.DMA((width // 16,))],
            "finish",
            {3: 0} if earlier else {},
        )(total, from_above, from_below, *earlier)

    *partial, _ = lax.optimization_barrier((*partial, edges[0]))
    weight_grad = call(
        gradient_kernel,
        array(entries * taps, cols),
        [whole(VMEM)] * PARTS,
        whole(VMEM),
        (),
        "gradient",
    )(*partial)
    return source.reshape(fields.shape), weight_grad.reshape(weights.shape)


def solution(mesh):
    return jax.shard_map(
        local,
        mesh=mesh,
        in_specs=(
            P("lev", "ens", "lat", "lon"),
            P("lev", "ens", "lat", "lon"),
            P("lev", "lat", "lon", "ens", None, None),
            P("lev", "lat", None, "ens", None),
            P("lev", "lat", "ens"),
        ),
        out_specs=(P("lev", "ens", "lat", "lon"), P("lev", "lat", "lon", "ens", None, None)),
        check_vma=False,
    )
```

```python
import functools

import jax
import jax.numpy as jnp
from jax import lax
from jax.experimental import pallas as pl
from jax.experimental.pallas import tpu as pltpu
from jax.sharding import PartitionSpec as P

HR = 2
CAP = 11
BASE = 8
SPARE = CAP - BASE
PARTS = 2
STRIDE = 16
TRASH = STRIDE - 2
COUNT = STRIDE - 1
BF16 = jnp.bfloat16
F32 = jnp.float32
VMEM = pltpu.VMEM
SMEM = pltpu.SMEM


def whole(space):
    return pl.BlockSpec(memory_space=space)


def wrap(value, size):
    return jnp.where(value < 0, value + size, value)


def prepare_kernel(bands, fields_hbm, rows_ref, *rest):
    *edges, held, wide, sems = rest
    rows, channels, _ = rows_ref.shape
    chunk = 16
    copies = []
    for i, c in enumerate(range(0, channels, chunk)):
        span = pl.ds(c * rows, chunk * rows)
        copies.append(pltpu.make_async_copy(fields_hbm.at[span], held.at[span], sems.at[i]))
        copies[-1].start()
    for i, c in enumerate(range(0, channels, chunk)):
        copies[i].wait()
        span = slice(c * rows, (c + chunk) * rows)
        wide[span] = held[span].astype(F32)
        for r in range(rows):
            rows_ref[r, c : c + chunk] = wide[pl.ds(c * rows + r, chunk, stride=rows), :].astype(BF16)
    if bands == 2:
        start = jnp.where(lax.axis_index("lat") == 0, rows - HR, 0)
        edges[0][...] = rows_ref[pl.ds(start, HR)]
    else:
        edges[0][...] = rows_ref[0:HR]
        edges[1][...] = rows_ref[rows - HR : rows]


def entry_of(lists_ref, number_ref, a, r, k, rows):
    used = k < number_ref[0, a, r]
    owner = jnp.where(used, lists_ref[0, a, 0, k, r], -1)
    return owner, HR + lists_ref[0, a, 1, k, r] * rows + lists_ref[0, a, 2, k, r]


def send_kernel(tiles, rows, per_row, lists_ref, number_ref, send_ref):
    me = lax.axis_index("lon")

    def scan(d):
        a = wrap(me + d - tiles, tiles)
        for s in range(CAP):
            send_ref[d * STRIDE + s] = rows + 2 * HR
        filled = jnp.int32(0)
        for r in range(rows):
            for k in range(per_row):
                owner, row = entry_of(lists_ref, number_ref, a, r, k, rows)
                send_ref[d * STRIDE + jnp.where(owner == me, filled, TRASH)] = row
                filled = filled + jnp.where(owner == me, 1, 0)
        send_ref[d * STRIDE + COUNT] = filled

    if tiles <= 4:
        for d in range(1, tiles):
            scan(d)
    else:
        pl.loop(1, tiles)(scan)


def pack_kernel(tiles, width, send_ref, rows_ref, before_ref, after_ref, ext_ref, *rest):
    n = tiles - 1
    middle = tiles // 2
    base, halves, spare = rest[: n - 1], rest[n - 1 : n - 1 + PARTS], rest[n - 1 + PARTS :]
    rows = rows_ref.shape[0]
    ext_ref[0:HR] = before_ref[...]
    ext_ref[HR : HR + rows] = rows_ref[...]
    ext_ref[HR + rows : HR + rows + HR] = after_ref[...]
    whole_distances = [d for d in range(1, tiles) if d != middle]
    for s in range(BASE):
        block = ext_ref[send_ref[middle * STRIDE + s]]
        for i in range(PARTS):
            halves[i][s] = block[i * width : (i + 1) * width]
    for d, out in zip(whole_distances, base):
        for s in range(BASE):
            out[s] = ext_ref[send_ref[d * STRIDE + s]]
    for d in range(1, tiles):

        @pl.when(send_ref[d * STRIDE + COUNT] > BASE)
        def _():
            for s in range(SPARE):
                spare[d - 1][s] = ext_ref[send_ref[d * STRIDE + BASE + s]]


def arrival_kernel(tiles, per_row, lists_ref, number_ref, cot_ref, taps_ref, *rest):
    cot_rows_ref, mix_ref, place_ref, own_ref, needed_ref, wide, taken = rest
    rows, channels, cols = cot_rows_ref.shape
    me = lax.axis_index("lon")
    entries = rows * per_row
    dump = rows + 2 * HR
    for s in range(CAP):
        own_ref[s] = dump

    def place(r, k, owner, row, d, count):
        used = owner >= 0
        own = owner == me
        slot = d * STRIDE + count
        source = jnp.where(own, tiles * STRIDE + row, slot)
        place_ref[r * per_row + k] = jnp.where(used, source, tiles * STRIDE + dump)
        place_ref[entries + r * per_row + k] = jnp.where(used, slot, tiles * STRIDE)
        own_ref[jnp.where(own, count, TRASH)] = row

    if tiles <= 4:

        def add_up(owner, counts):
            return [count + jnp.where(owner == o, 1, 0) for o, count in enumerate(counts)]

        most = jnp.int32(0)
        for d in range(1, tiles):
            a = wrap(me + d - tiles, tiles)
            counts = [jnp.int32(0)] * tiles
            for r in range(rows):
                for k in range(per_row):
                    counts = add_up(entry_of(lists_ref, number_ref, a, r, k, rows)[0], counts)
            for o in range(tiles):
                most = jnp.maximum(most, jnp.where(a == o, 0, counts[o]))
        counts = [jnp.int32(0)] * tiles
        for r in range(rows):
            for k in range(per_row):
                owner, row = entry_of(lists_ref, number_ref, me, r, k, rows)
                count = sum(jnp.where(owner == o, counts[o], 0) for o in range(tiles))
                place(r, k, owner, row, wrap(me - owner, tiles), count)
                counts = add_up(owner, counts)
        for o in range(tiles):
            place_ref[2 * entries + wrap(me - o, tiles)] = counts[o]
            most = jnp.maximum(most, jnp.where(me == o, 0, counts[o]))
        needed_ref[0] = jnp.where(most > BASE, 1, 0)
    else:
        for d in range(tiles + 1):
            taken[d] = 0

        @pl.loop(0, rows)
        def _(r):
            for k in range(per_row):
                owner, row = entry_of(lists_ref, number_ref, me, r, k, rows)
                d = jnp.where(owner >= 0, wrap(me - owner, tiles), tiles)
                place(r, k, owner, row, d, taken[d])
                taken[d] = taken[d] + 1

        for d in range(tiles):
            place_ref[2 * entries + d] = taken[d]
        needed_ref[0] = 0

    wide[...] = cot_ref[...].astype(F32)
    for r in range(rows):
        cot_rows_ref[r] = wide[pl.ds(r, channels, stride=rows), :].astype(BF16)
    w0, w1, w2, w3 = (taps_ref[j] for j in range(4))
    cell = lax.broadcasted_iota(jnp.int32, w0.shape, 1)
    first, last, late = cell == 0, cell == cols - 1, cell == cols - 2
    mix_ref[0] = pltpu.roll(jnp.where(first, 0.0, w0), cols - 1, 1)
    mix_ref[1] = w1 + jnp.where(first, w0, 0.0) + jnp.where(last, w2 + w3, 0.0)
    mix_ref[2] = pltpu.roll(jnp.where(last, 0.0, w2) + jnp.where(late, w3, 0.0), 1, 1)
    mix_ref[3] = pltpu.roll(jnp.where(last | late, 0.0, w3), 2, 1)


def compute_kernel(tiles, per_row, start, width, place_ref, mix_ref, cot_ref, ext_ref, *rest):
    n = tiles - 1
    middle = tiles // 2
    whole_distances = [d for d in range(1, tiles) if d != middle]
    base, half, spare, rest = rest[: n - 1], rest[n - 1], rest[n : 2 * n], rest[2 * n :]
    if start > 0:
        rest = rest[2 * n :]
    own_out, base_out, spare_out, rest = rest[0], rest[1:n], rest[n : 2 * n], rest[2 * n :]
    half_out, grad_ref, blocks, terms = rest
    rows, _, cols = cot_ref.shape
    entries = rows * per_row
    ext = rows + 2 * HR
    part = min(width, 32)
    mine = slice(start, start + width)
    blocks[tiles * STRIDE : tiles * STRIDE + ext] = ext_ref[0:ext, mine]
    blocks[tiles * STRIDE + ext] = jnp.zeros((width, cols), BF16)
    blocks[middle * STRIDE : middle * STRIDE + BASE] = half[...]
    for d, arrived in zip(whole_distances, base):
        blocks[d * STRIDE : d * STRIDE + BASE] = arrived[:, mine]
    for d in range(1, tiles):

        @pl.when(place_ref[2 * entries + d] > BASE)
        def _():
            blocks[d * STRIDE + BASE : d * STRIDE + CAP] = spare[d - 1][:, mine]

    def row(r, _):
        source = [place_ref[r * per_row + k] for k in range(per_row)]
        target = [place_ref[entries + r * per_row + k] for k in range(per_row)]
        mix = [[mix_ref[j, pl.ds(r * per_row + k, 1), :] for j in range(4)] for k in range(per_row)]
        for lo in range(0, width, part):
            block = [blocks[source[k], lo : lo + part].astype(F32) for k in range(per_row)]
            tap = [sum(block[k] * mix[k][j] for k in range(per_row)) for j in range(4)]
            interp = (tap[1] + pltpu.roll(tap[0], 1, 1)) + (
                pltpu.roll(tap[2], cols - 1, 1) + pltpu.roll(tap[3], cols - 2, 1)
            )
            bent = jnp.tanh(interp)
            scaled = cot_ref[r, start + lo : start + lo + part].astype(F32) * (2.0 - bent * bent)
            scaled = scaled.astype(BF16).astype(F32)
            moved = [
                pltpu.roll(scaled, cols - 1, 1),
                scaled,
                pltpu.roll(scaled, 1, 1),
                pltpu.roll(scaled, 2, 1),
            ]
            for k in range(per_row):
                term = (moved[0] * mix[k][0] + moved[1] * mix[k][1]) + (
                    moved[2] * mix[k][2] + moved[3] * mix[k][3]
                )
                terms[target[k], lo : lo + part] = term.astype(BF16)
                for j in range(4):
                    at = (r * per_row + k) * 4 + j
                    product = jnp.sum((block[k] * moved[j]).reshape(part // 8, 8, cols), axis=0)
                    grad_ref[at] = product if lo == 0 else grad_ref[at] + product
        return 0

    lax.fori_loop(0, rows, row, 0, unroll=4)
    half_out[...] = terms[middle * STRIDE : middle * STRIDE + BASE]
    for d, out in zip(whole_distances, base_out):
        out[:, mine] = terms[d * STRIDE : d * STRIDE + BASE]
    for d in range(1, tiles):

        @pl.when(place_ref[2 * entries + d] > BASE)
        def _():
            spare_out[d - 1][:, mine] = terms[d * STRIDE + BASE : d * STRIDE + CAP]

    own_out[:, mine] = terms[0:CAP]


def gradient_kernel(*refs):
    *partial_refs, out_ref = refs
    sums = jnp.sum(sum(ref[...] for ref in partial_refs), axis=1)
    count, cols = sums.shape
    tap = lax.broadcasted_iota(jnp.int32, sums.shape, 0) & 3
    cell = lax.broadcasted_iota(jnp.int32, sums.shape, 1)
    grads = jnp.where(tap == 0, pltpu.roll(sums, 1, 1), sums)
    grads = jnp.where(tap == 2, pltpu.roll(sums, cols - 1, 1), grads)
    grads = jnp.where(tap == 3, pltpu.roll(sums, cols - 2, 1), grads)
    following = pltpu.roll(grads, count - 1, 0)
    previous = pltpu.roll(grads, 1, 0)
    second = pltpu.roll(grads, 2, 0)
    fixed = jnp.where((tap == 0) & (cell == 0), following, grads)
    fixed = jnp.where((tap == 2) & (cell == cols - 1), previous, fixed)
    fixed = jnp.where((tap == 3) & (cell == cols - 2), previous, fixed)
    fixed = jnp.where((tap == 3) & (cell == cols - 1), second, fixed)
    out_ref[...] = fixed.astype(BF16)


def add_own_kernel(table_ref, own_ref, total_ref):
    total_ref[...] = jnp.zeros_like(total_ref)
    for s in range(CAP):
        at = table_ref[s]
        total_ref[at] = total_ref[at] + own_ref[s].astype(F32)


def slot_refs(tiles, base, halves, spare):
    middle = tiles // 2
    whole_distances = [d for d in range(1, tiles) if d != middle]
    out = [(d, 0, BASE, 0, ref) for d, ref in zip(whole_distances, base)]
    width = halves[0].shape[1]
    out += [(middle, 0, BASE, i * width, ref) for i, ref in enumerate(halves)]
    return out, [(d, BASE, SPARE, 0, ref) for d, ref in enumerate(spare, 1)]


def edge_kernel(tiles, bands, send_ref, total_ref, *rest):
    n = tiles - 1
    base, halves, spare, edges = rest[: n - 1], rest[n - 1 : n - 1 + PARTS], rest[n - 1 + PARTS : 2 * n - 1 + PARTS], rest[2 * n - 1 + PARTS :]
    *edges, sums = edges
    ext = total_ref.shape[0] - 1
    if bands == 2:
        starts = [jnp.where(lax.axis_index("lat") == 0, ext - HR, 0)]
    else:
        starts = [0, ext - HR]
    always, seldom = slot_refs(tiles, base, halves, spare)
    wanted = [(e, h) for e in range(len(starts)) for h in range(HR)]
    for e, h in wanted:
        sums[e, h] = total_ref[starts[e] + h]

    def gather(refs):
        for d, first, slots, channel, ref in refs:
            part = slice(channel, channel + ref.shape[1])
            for c in range(part.start, part.stop, 16):
                found = [sums[e, h, c : c + 16] for e, h in wanted]
                for s in range(slots):
                    at = send_ref[d * STRIDE + first + s]
                    value = ref[s, c - channel : c - channel + 16].astype(F32)
                    found = [
                        jnp.where(at == starts[e] + h, total + value, total)
                        for (e, h), total in zip(wanted, found)
                    ]
                for (e, h), total in zip(wanted, found):
                    sums[e, h, c : c + 16] = total

    gather(always)
    for item in seldom:

        @pl.when(send_ref[item[0] * STRIDE + COUNT] > BASE)
        def _():
            gather([item])

    for e, edge in enumerate(edges):
        edge[...] = sums[e].astype(BF16)


def add_kernel(tiles, send_ref, _, *rest):
    n = tiles - 1
    base, halves, spare, (total_ref,) = rest[: n - 1], rest[n - 1 : n - 1 + PARTS], rest[n - 1 + PARTS : 2 * n - 1 + PARTS], rest[2 * n - 1 + PARTS :]
    always, seldom = slot_refs(tiles, base, halves, spare)

    def gather(d, first, slots, channel, ref):
        part = slice(channel, channel + ref.shape[1])
        for s in range(slots):
            at = send_ref[d * STRIDE + first + s]
            total_ref[at, part] = total_ref[at, part] + ref[s].astype(F32)

    for item in always:
        gather(*item)
    for item in seldom:
        pl.when(send_ref[item[0] * STRIDE + COUNT] > BASE)(functools.partial(gather, *item))


def finish_kernel(bands, rows, total_ref, above_ref, below_ref, out_hbm, held, sems):
    channels = total_ref.shape[1]
    band = lax.axis_index("lat")
    chunk = 16
    copies = []
    for i, c in enumerate(range(0, channels, chunk)):
        part = slice(c, c + chunk)
        for r in range(rows):
            value = total_ref[HR + r, part]
            if r < HR:
                value = value + jnp.where(band > 0, above_ref[r, part].astype(F32), 0.0)
            if r >= rows - HR:
                below = below_ref[r - rows + HR, part].astype(F32)
                value = value + jnp.where(band < bands - 1, below, 0.0)
            held[pl.ds(c * rows + r, chunk, stride=rows), :] = value
        source = held.at[pl.ds(c * rows, chunk * rows)]
        target = out_hbm.at[pl.ds(c * rows, chunk * rows)]
        copies.append(pltpu.make_async_copy(source, target, sems.at[i]))
        copies[-1].start()
    for copy in copies:
        copy.wait()


def swap_lat(edges, bands):
    if bands == 2:
        got = lax.ppermute(edges[0], "lat", [(0, 1), (1, 0)])
        return got, got
    down = [(i, i + 1) for i in range(bands - 1)]
    up = [(i + 1, i) for i in range(bands - 1)]
    return lax.ppermute(edges[1], "lat", down), lax.ppermute(edges[0], "lat", up)


def local(fields, arrival_cot, weights, departures, counts):
    lev_dev, field_count, rows, cols = fields.shape
    channels = lev_dev * field_count
    tiles = lax.axis_size("lon")
    bands = lax.axis_size("lat")
    per_row, taps = weights.shape[3], weights.shape[4]
    entries = rows * per_row
    ext = rows + 2 * HR
    partners = tiles - 1
    middle = tiles // 2
    whole_distances = [d for d in range(1, tiles) if d != middle]
    width = channels // PARTS
    params = pltpu.CompilerParams(vmem_limit_bytes=48 * 1024 * 1024)

    def call(kernel, out_shape, in_specs, out_specs, scratch=(), name=None, aliases={}):
        return pl.pallas_call(
            kernel,
            out_shape=out_shape,
            in_specs=in_specs,
            out_specs=out_specs,
            scratch_shapes=list(scratch),
            compiler_params=params,
            input_output_aliases=aliases,
            name=name,
        )

    def array(*shape, dtype=BF16):
        return jax.ShapeDtypeStruct(shape, dtype)

    def move(part, d):
        return lax.ppermute(part, "lon", [(i, (i + d) % tiles) for i in range(tiles)])

    def move_all(parts, sign):
        return [move(part, sign * d) for d, part in enumerate(parts, 1)]

    def move_spare(parts, sign):
        return lax.cond(needed, lambda parts: move_all(parts, sign), lambda parts: parts, list(parts))

    def move_whole(parts, sign):
        return [move(part, sign * d) for d, part in zip(whole_distances, parts)]

    lists = jnp.transpose(departures, (0, 2, 4, 3, 1))
    number = jnp.transpose(counts, (0, 2, 1))

    edge_count = 1 if bands == 2 else 2
    edge = (array(HR, channels, cols),) * edge_count
    base_slots = (array(BASE, channels, cols),) * (partners - 1)
    half_slots = array(BASE, width, cols)
    spare_slots = (array(SPARE, channels, cols),) * partners

    def hbm(value):
        return pltpu.with_memory_space_constraint(value, pltpu.HBM)

    row_blocks, *edges = call(
        functools.partial(prepare_kernel, bands),
        (array(rows, channels, cols),) + edge,
        [whole(pltpu.HBM)],
        (whole(VMEM),) * (1 + edge_count),
        [
            VMEM((channels * rows, cols), BF16),
            VMEM((channels * rows, cols), F32),
            pltpu.SemaphoreType.DMA((channels // 16,)),
        ],
        "prepare",
    )(hbm(fields.reshape(channels * rows, cols)))
    before, after = swap_lat(edges, bands)

    send_rows = call(
        functools.partial(send_kernel, tiles, rows, per_row),
        array(tiles * STRIDE, dtype=jnp.int32),
        [whole(SMEM)] * 2,
        whole(SMEM),
        (),
        "send",
    )(lists, number)
    ext_blocks, *rest = call(
        functools.partial(pack_kernel, tiles, width),
        (array(ext + 1, channels, cols),) + base_slots + (half_slots,) * PARTS + spare_slots,
        [whole(SMEM)] + [whole(VMEM)] * 3,
        (whole(VMEM),) * (2 * partners + PARTS),
        (),
        "pack",
    )(send_rows, row_blocks, before, after)
    base, halves, spare = (
        rest[: partners - 1],
        rest[partners - 1 : partners - 1 + PARTS],
        rest[partners - 1 + PARTS :],
    )
    halves = [move(half, middle) for half in halves]
    base = move_whole(base, 1)

    mixing = weights.reshape(rows, per_row, taps, cols).astype(F32)
    mixing = jnp.transpose(mixing, (2, 0, 1, 3)).reshape(taps, entries, cols)
    cot_rows, mix, places, own_table, needed = call(
        functools.partial(arrival_kernel, tiles, per_row),
        (
            array(rows, channels, cols),
            array(taps, entries, cols, dtype=F32),
            array(2 * entries + tiles, dtype=jnp.int32),
            array(STRIDE, dtype=jnp.int32),
            array(1, dtype=jnp.int32),
        ),
        [whole(SMEM), whole(SMEM), whole(VMEM), whole(VMEM)],
        (whole(VMEM), whole(VMEM), whole(SMEM), whole(SMEM), whole(SMEM)),
        [VMEM((channels * rows, cols), F32), SMEM((tiles + 1,), jnp.int32)],
        "arrival",
    )(lists, number, arrival_cot.reshape(channels * rows, cols), mixing)
    if tiles <= 4:
        needed = needed[0] > 0
    else:
        tile = jnp.arange(tiles, dtype=jnp.int32)
        entry = jnp.arange(per_row, dtype=jnp.int32)
        named = (entry[:, None] < number[0][:, None, :]) & (lists[0, :, 0] == tile[:, None, None, None])
        filled = jnp.sum(jnp.where(named, 1, 0), axis=(2, 3))
        needed = jnp.any((filled > BASE) & (tile[None, :] != tile[:, None]))
    spare = move_spare(spare, 1)

    filling = (array(CAP, channels, cols),) + base_slots + spare_slots
    began, back, partial = [], [], []
    for i in range(PARTS):
        inputs = 4 + 2 * partners
        *began, half, sums = call(
            functools.partial(compute_kernel, tiles, per_row, i * width, width),
            filling + (half_slots, array(entries * taps, 8, cols, dtype=F32)),
            [whole(SMEM)] + [whole(VMEM)] * (inputs - 1 + len(began)),
            (whole(VMEM),) * (len(filling) + 2),
            [
                VMEM((tiles * STRIDE + ext + 1, width, cols), BF16),
                VMEM((tiles * STRIDE + 1, width, cols), BF16),
            ],
            "compute",
            {inputs + j: j for j in range(len(began))},
        )(places, mix, cot_rows, ext_blocks, *base, halves[i], *spare, *began)
        back.append(move(half, -middle))
        partial.append(sums)
    own, base, spare = began[0], move_whole(began[1:partners], -1), move_spare(began[partners:], -1)

    sums = array(ext + 1, channels, cols, dtype=F32)
    total = call(add_own_kernel, sums, [whole(SMEM), whole(VMEM)], whole(VMEM), (), "add_own")(
        own_table, own
    )
    returned = [*base, *back, *spare]
    edges = call(
        functools.partial(edge_kernel, tiles, bands),
        edge,
        [whole(SMEM)] + [whole(VMEM)] * (1 + len(returned)),
        (whole(VMEM),) * edge_count,
        [VMEM((edge_count, HR, channels, cols), F32)],
        "edges",
    )(send_rows, total, *returned)
    from_above, from_below = swap_lat(edges, bands)
    total = call(
        functools.partial(add_kernel, tiles),
        sums,
        [whole(SMEM)] + [whole(VMEM)] * (1 + len(returned)),
        whole(VMEM),
        (),
        "add",
        {1: 0},
    )(send_rows, lax.optimization_barrier((total, edges[0]))[0], *returned)
    source = call(
        functools.partial(finish_kernel, bands, rows),
        array(channels * rows, cols, dtype=F32),
        [whole(VMEM)] * 3,
        whole(pltpu.HBM),
        [VMEM((channels * rows, cols), F32), pltpu.SemaphoreType.DMA((channels // 16,))],
        "finish",
    )(total, from_above, from_below)

    *partial, _ = lax.optimization_barrier((*partial, edges[0]))
    weight_grad = call(
        gradient_kernel,
        array(entries * taps, cols),
        [whole(VMEM)] * PARTS,
        whole(VMEM),
        (),
        "gradient",
    )(*partial)
    return source.reshape(fields.shape), weight_grad.reshape(weights.shape)


def solution(mesh):
    return jax.shard_map(
        local,
        mesh=mesh,
        in_specs=(
            P("lev", "ens", "lat", "lon"),
            P("lev", "ens", "lat", "lon"),
            P("lev", "lat", "lon", "ens", None, None),
            P("lev", "lat", None, "ens", None),
            P("lev", "lat", "ens"),
        ),
        out_specs=(P("lev", "ens", "lat", "lon"), P("lev", "lat", "lon", "ens", None, None)),
        check_vma=False,
    )
```

```python
import functools

import jax
import jax.numpy as jnp
from jax import lax
from jax.experimental import pallas as pl
from jax.experimental.pallas import tpu as pltpu
from jax.sharding import PartitionSpec as P

HR = 2
CAP = 11
BASE = 8
SPARE = CAP - BASE
PARTS = 1
STRIDE = 16
TRASH = STRIDE - 2
COUNT = STRIDE - 1
BF16 = jnp.bfloat16
F32 = jnp.float32
VMEM = pltpu.VMEM
SMEM = pltpu.SMEM


def whole(space):
    return pl.BlockSpec(memory_space=space)


def wrap(value, size):
    return jnp.where(value < 0, value + size, value)


def prepare_kernel(bands, fields_hbm, rows_ref, *rest):
    *edges, held, wide, sems = rest
    rows, channels, _ = rows_ref.shape
    chunk = 16
    copies = []
    for i, c in enumerate(range(0, channels, chunk)):
        span = pl.ds(c * rows, chunk * rows)
        copies.append(pltpu.make_async_copy(fields_hbm.at[span], held.at[span], sems.at[i]))
        copies[-1].start()
    for i, c in enumerate(range(0, channels, chunk)):
        copies[i].wait()
        span = slice(c * rows, (c + chunk) * rows)
        wide[span] = held[span].astype(F32)
        for r in range(rows):
            rows_ref[r, c : c + chunk] = wide[pl.ds(c * rows + r, chunk, stride=rows), :].astype(BF16)
    if bands == 2:
        start = jnp.where(lax.axis_index("lat") == 0, rows - HR, 0)
        edges[0][...] = rows_ref[pl.ds(start, HR)]
    else:
        edges[0][...] = rows_ref[0:HR]
        edges[1][...] = rows_ref[rows - HR : rows]


def entry_of(lists_ref, number_ref, a, r, k, rows):
    used = k < number_ref[0, a, r]
    owner = jnp.where(used, lists_ref[0, a, 0, k, r], -1)
    return owner, HR + lists_ref[0, a, 1, k, r] * rows + lists_ref[0, a, 2, k, r]


def add_up(owner, counts):
    return [count + jnp.where(owner == o, 1, 0) for o, count in enumerate(counts)]


def send_kernel(tiles, rows, per_row, lists_ref, number_ref, send_ref):
    me = lax.axis_index("lon")

    def scan(d, most):
        a = wrap(me + d - tiles, tiles)
        for s in range(CAP):
            send_ref[d * STRIDE + s] = rows + 2 * HR
        filled = jnp.int32(0)
        others = [o for o in range(1, tiles) if o != d] if tiles <= 4 else []
        owners = [wrap(me + o - tiles, tiles) for o in others]
        counts = [jnp.int32(0)] * len(others)
        for r in range(rows):
            for k in range(per_row):
                owner, row = entry_of(lists_ref, number_ref, a, r, k, rows)
                hit = owner == me
                send_ref[d * STRIDE + jnp.where(hit, filled, TRASH)] = row
                filled = filled + jnp.where(hit, 1, 0)
                counts = [count + jnp.where(owner == o, 1, 0) for o, count in zip(owners, counts)]
        send_ref[d * STRIDE + COUNT] = filled
        for count in [filled] + counts:
            most = jnp.maximum(most, count)
        return most

    if tiles <= 4:
        most = jnp.int32(0)
        for d in range(1, tiles):
            most = scan(d, most)
        send_ref[COUNT] = most
    else:

        @pl.loop(1, tiles)
        def _(d):
            scan(d, jnp.int32(0))


def pack_kernel(tiles, width, send_ref, rows_ref, before_ref, after_ref, ext_ref, *rest):
    n = tiles - 1
    middle = tiles // 2
    base, halves, spare = rest[: n - 1], rest[n - 1 : n - 1 + PARTS], rest[n - 1 + PARTS :]
    rows = rows_ref.shape[0]
    ext_ref[0:HR] = before_ref[...]
    ext_ref[HR : HR + rows] = rows_ref[...]
    ext_ref[HR + rows : HR + rows + HR] = after_ref[...]
    whole_distances = [d for d in range(1, tiles) if d != middle]
    for s in range(BASE):
        block = ext_ref[send_ref[middle * STRIDE + s]]
        for i in range(PARTS):
            halves[i][s] = block[i * width : (i + 1) * width]
    for d, out in zip(whole_distances, base):
        for s in range(BASE):
            out[s] = ext_ref[send_ref[d * STRIDE + s]]
    for d in range(1, tiles):

        @pl.when(send_ref[d * STRIDE + COUNT] > BASE)
        def _():
            for s in range(SPARE):
                spare[d - 1][s] = ext_ref[send_ref[d * STRIDE + BASE + s]]


def arrival_kernel(tiles, per_row, send_ref, lists_ref, number_ref, cot_ref, taps_ref, *rest):
    cot_rows_ref, mix_ref, place_ref, own_ref, needed_ref, wide, taken = rest
    rows, channels, cols = cot_rows_ref.shape
    me = lax.axis_index("lon")
    entries = rows * per_row
    dump = rows + 2 * HR
    for s in range(CAP):
        own_ref[s] = dump

    def place(r, k, owner, row, d, count):
        used = owner >= 0
        own = owner == me
        slot = d * STRIDE + count
        source = jnp.where(own, tiles * STRIDE + row, slot)
        place_ref[r * per_row + k] = jnp.where(used, source, tiles * STRIDE + dump)
        place_ref[entries + r * per_row + k] = jnp.where(used, slot, tiles * STRIDE)
        own_ref[jnp.where(own, count, TRASH)] = row

    if tiles <= 4:
        most = send_ref[COUNT]
        counts = [jnp.int32(0)] * tiles
        for r in range(rows):
            for k in range(per_row):
                owner, row = entry_of(lists_ref, number_ref, me, r, k, rows)
                count = sum(jnp.where(owner == o, counts[o], 0) for o in range(tiles))
                place(r, k, owner, row, wrap(me - owner, tiles), count)
                counts = add_up(owner, counts)
        for o in range(tiles):
            place_ref[2 * entries + wrap(me - o, tiles)] = counts[o]
            most = jnp.maximum(most, jnp.where(me == o, 0, counts[o]))
        needed_ref[0] = jnp.where(most > BASE, 1, 0)
    else:
        for d in range(tiles + 1):
            taken[d] = 0

        @pl.loop(0, rows)
        def _(r):
            for k in range(per_row):
                owner, row = entry_of(lists_ref, number_ref, me, r, k, rows)
                d = jnp.where(owner >= 0, wrap(me - owner, tiles), tiles)
                place(r, k, owner, row, d, taken[d])
                taken[d] = taken[d] + 1

        for d in range(tiles):
            place_ref[2 * entries + d] = taken[d]
        needed_ref[0] = 0

    wide[...] = cot_ref[...].astype(F32)
    for r in range(rows):
        cot_rows_ref[r] = wide[pl.ds(r, channels, stride=rows), :].astype(BF16)
    w0, w1, w2, w3 = (taps_ref[j] for j in range(4))
    cell = lax.broadcasted_iota(jnp.int32, w0.shape, 1)
    first, last, late = cell == 0, cell == cols - 1, cell == cols - 2
    mix_ref[0] = pltpu.roll(jnp.where(first, 0.0, w0), cols - 1, 1)
    mix_ref[1] = w1 + jnp.where(first, w0, 0.0) + jnp.where(last, w2 + w3, 0.0)
    mix_ref[2] = pltpu.roll(jnp.where(last, 0.0, w2) + jnp.where(late, w3, 0.0), 1, 1)
    mix_ref[3] = pltpu.roll(jnp.where(last | late, 0.0, w3), 2, 1)


def compute_kernel(tiles, per_row, start, width, place_ref, mix_ref, cot_ref, ext_ref, *rest):
    n = tiles - 1
    middle = tiles // 2
    whole_distances = [d for d in range(1, tiles) if d != middle]
    base, half, spare, rest = rest[: n - 1], rest[n - 1], rest[n : 2 * n], rest[2 * n :]
    if start > 0:
        rest = rest[2 * n :]
    own_out, base_out, spare_out, rest = rest[0], rest[1:n], rest[n : 2 * n], rest[2 * n :]
    half_out, grad_ref, blocks, terms = rest
    rows, _, cols = cot_ref.shape
    entries = rows * per_row
    ext = rows + 2 * HR
    part = min(width, 32)
    mine = slice(start, start + width)
    blocks[tiles * STRIDE : tiles * STRIDE + ext] = ext_ref[0:ext, mine]
    blocks[tiles * STRIDE + ext] = jnp.zeros((width, cols), BF16)
    blocks[middle * STRIDE : middle * STRIDE + BASE] = half[...]
    for d, arrived in zip(whole_distances, base):
        blocks[d * STRIDE : d * STRIDE + BASE] = arrived[:, mine]
    for d in range(1, tiles):

        @pl.when(place_ref[2 * entries + d] > BASE)
        def _():
            blocks[d * STRIDE + BASE : d * STRIDE + CAP] = spare[d - 1][:, mine]

    def row(r, _):
        source = [place_ref[r * per_row + k] for k in range(per_row)]
        target = [place_ref[entries + r * per_row + k] for k in range(per_row)]
        mix = [[mix_ref[j, pl.ds(r * per_row + k, 1), :] for j in range(4)] for k in range(per_row)]
        for lo in range(0, width, part):
            block = [blocks[source[k], lo : lo + part].astype(F32) for k in range(per_row)]
            tap = [sum(block[k] * mix[k][j] for k in range(per_row)) for j in range(4)]
            interp = (tap[1] + pltpu.roll(tap[0], 1, 1)) + (
                pltpu.roll(tap[2], cols - 1, 1) + pltpu.roll(tap[3], cols - 2, 1)
            )
            bent = jnp.tanh(interp)
            scaled = cot_ref[r, start + lo : start + lo + part].astype(F32) * (2.0 - bent * bent)
            scaled = scaled.astype(BF16).astype(F32)
            moved = [
                pltpu.roll(scaled, cols - 1, 1),
                scaled,
                pltpu.roll(scaled, 1, 1),
                pltpu.roll(scaled, 2, 1),
            ]
            for k in range(per_row):
                term = (moved[0] * mix[k][0] + moved[1] * mix[k][1]) + (
                    moved[2] * mix[k][2] + moved[3] * mix[k][3]
                )
                terms[target[k], lo : lo + part] = term.astype(BF16)
                for j in range(4):
                    at = (r * per_row + k) * 4 + j
                    product = jnp.sum((block[k] * moved[j]).reshape(part // 8, 8, cols), axis=0)
                    grad_ref[at] = product if lo == 0 else grad_ref[at] + product
        return 0

    lax.fori_loop(0, rows, row, 0, unroll=4)
    half_out[...] = terms[middle * STRIDE : middle * STRIDE + BASE]
    for d, out in zip(whole_distances, base_out):
        out[:, mine] = terms[d * STRIDE : d * STRIDE + BASE]
    for d in range(1, tiles):

        @pl.when(place_ref[2 * entries + d] > BASE)
        def _():
            spare_out[d - 1][:, mine] = terms[d * STRIDE + BASE : d * STRIDE + CAP]

    own_out[:, mine] = terms[0:CAP]


def gradient_kernel(*refs):
    *partial_refs, out_ref = refs
    sums = jnp.sum(sum(ref[...] for ref in partial_refs), axis=1)
    count, cols = sums.shape
    tap = lax.broadcasted_iota(jnp.int32, sums.shape, 0) & 3
    cell = lax.broadcasted_iota(jnp.int32, sums.shape, 1)
    grads = jnp.where(tap == 0, pltpu.roll(sums, 1, 1), sums)
    grads = jnp.where(tap == 2, pltpu.roll(sums, cols - 1, 1), grads)
    grads = jnp.where(tap == 3, pltpu.roll(sums, cols - 2, 1), grads)
    following = pltpu.roll(grads, count - 1, 0)
    previous = pltpu.roll(grads, 1, 0)
    second = pltpu.roll(grads, 2, 0)
    fixed = jnp.where((tap == 0) & (cell == 0), following, grads)
    fixed = jnp.where((tap == 2) & (cell == cols - 1), previous, fixed)
    fixed = jnp.where((tap == 3) & (cell == cols - 2), previous, fixed)
    fixed = jnp.where((tap == 3) & (cell == cols - 1), second, fixed)
    out_ref[...] = fixed.astype(BF16)


def add_own_kernel(table_ref, own_ref, total_ref):
    total_ref[...] = jnp.zeros_like(total_ref)
    for s in range(CAP):
        at = table_ref[s]
        total_ref[at] = total_ref[at] + own_ref[s].astype(F32)


def slot_refs(tiles, base, halves, spare):
    middle = tiles // 2
    whole_distances = [d for d in range(1, tiles) if d != middle]
    out = [(d, 0, BASE, 0, ref) for d, ref in zip(whole_distances, base)]
    width = halves[0].shape[1]
    out += [(middle, 0, BASE, i * width, ref) for i, ref in enumerate(halves)]
    return out, [(d, BASE, SPARE, 0, ref) for d, ref in enumerate(spare, 1)]


def edge_kernel(tiles, bands, send_ref, total_ref, *rest):
    n = tiles - 1
    base, halves, spare, edges = rest[: n - 1], rest[n - 1 : n - 1 + PARTS], rest[n - 1 + PARTS : 2 * n - 1 + PARTS], rest[2 * n - 1 + PARTS :]
    *edges, sums = edges
    ext = total_ref.shape[0] - 1
    if bands == 2:
        starts = [jnp.where(lax.axis_index("lat") == 0, ext - HR, 0)]
    else:
        starts = [0, ext - HR]
    always, seldom = slot_refs(tiles, base, halves, spare)
    wanted = [(e, h) for e in range(len(starts)) for h in range(HR)]
    for e, h in wanted:
        sums[e, h] = total_ref[starts[e] + h]

    def gather(refs):
        for d, first, slots, channel, ref in refs:
            part = slice(channel, channel + ref.shape[1])
            for c in range(part.start, part.stop, 16):
                found = [sums[e, h, c : c + 16] for e, h in wanted]
                for s in range(slots):
                    at = send_ref[d * STRIDE + first + s]
                    value = ref[s, c - channel : c - channel + 16].astype(F32)
                    found = [
                        jnp.where(at == starts[e] + h, total + value, total)
                        for (e, h), total in zip(wanted, found)
                    ]
                for (e, h), total in zip(wanted, found):
                    sums[e, h, c : c + 16] = total

    gather(always)
    for item in seldom:

        @pl.when(send_ref[item[0] * STRIDE + COUNT] > BASE)
        def _():
            gather([item])

    for e, edge in enumerate(edges):
        edge[...] = sums[e].astype(BF16)


def add_kernel(tiles, send_ref, _, *rest):
    n = tiles - 1
    base, halves, spare, (total_ref,) = rest[: n - 1], rest[n - 1 : n - 1 + PARTS], rest[n - 1 + PARTS : 2 * n - 1 + PARTS], rest[2 * n - 1 + PARTS :]
    always, seldom = slot_refs(tiles, base, halves, spare)

    def gather(d, first, slots, channel, ref):
        part = slice(channel, channel + ref.shape[1])
        for s in range(slots):
            at = send_ref[d * STRIDE + first + s]
            total_ref[at, part] = total_ref[at, part] + ref[s].astype(F32)

    for item in always:
        gather(*item)
    for item in seldom:
        pl.when(send_ref[item[0] * STRIDE + COUNT] > BASE)(functools.partial(gather, *item))


def finish_kernel(bands, rows, total_ref, above_ref, below_ref, out_hbm, held, sems):
    channels = total_ref.shape[1]
    band = lax.axis_index("lat")
    chunk = 16
    copies = []
    for i, c in enumerate(range(0, channels, chunk)):
        part = slice(c, c + chunk)
        for r in range(rows):
            value = total_ref[HR + r, part]
            if r < HR:
                value = value + jnp.where(band > 0, above_ref[r, part].astype(F32), 0.0)
            if r >= rows - HR:
                below = below_ref[r - rows + HR, part].astype(F32)
                value = value + jnp.where(band < bands - 1, below, 0.0)
            held[pl.ds(c * rows + r, chunk, stride=rows), :] = value
        source = held.at[pl.ds(c * rows, chunk * rows)]
        target = out_hbm.at[pl.ds(c * rows, chunk * rows)]
        copies.append(pltpu.make_async_copy(source, target, sems.at[i]))
        copies[-1].start()
    for copy in copies:
        copy.wait()


def swap_lat(edges, bands):
    if bands == 2:
        got = lax.ppermute(edges[0], "lat", [(0, 1), (1, 0)])
        return got, got
    down = [(i, i + 1) for i in range(bands - 1)]
    up = [(i + 1, i) for i in range(bands - 1)]
    return lax.ppermute(edges[1], "lat", down), lax.ppermute(edges[0], "lat", up)


def local(fields, arrival_cot, weights, departures, counts):
    lev_dev, field_count, rows, cols = fields.shape
    channels = lev_dev * field_count
    tiles = lax.axis_size("lon")
    bands = lax.axis_size("lat")
    per_row, taps = weights.shape[3], weights.shape[4]
    entries = rows * per_row
    ext = rows + 2 * HR
    partners = tiles - 1
    middle = tiles // 2
    whole_distances = [d for d in range(1, tiles) if d != middle]
    width = channels // PARTS
    params = pltpu.CompilerParams(vmem_limit_bytes=48 * 1024 * 1024)

    def call(kernel, out_shape, in_specs, out_specs, scratch=(), name=None, aliases={}):
        return pl.pallas_call(
            kernel,
            out_shape=out_shape,
            in_specs=in_specs,
            out_specs=out_specs,
            scratch_shapes=list(scratch),
            compiler_params=params,
            input_output_aliases=aliases,
            name=name,
        )

    def array(*shape, dtype=BF16):
        return jax.ShapeDtypeStruct(shape, dtype)

    def move(part, d):
        return lax.ppermute(part, "lon", [(i, (i + d) % tiles) for i in range(tiles)])

    def move_all(parts, sign):
        return [move(part, sign * d) for d, part in enumerate(parts, 1)]

    def move_spare(parts, sign):
        return lax.cond(needed, lambda parts: move_all(parts, sign), lambda parts: parts, list(parts))

    def move_whole(parts, sign):
        return [move(part, sign * d) for d, part in zip(whole_distances, parts)]

    lists = jnp.transpose(departures, (0, 2, 4, 3, 1))
    number = jnp.transpose(counts, (0, 2, 1))

    edge_count = 1 if bands == 2 else 2
    edge = (array(HR, channels, cols),) * edge_count
    base_slots = (array(BASE, channels, cols),) * (partners - 1)
    half_slots = array(BASE, width, cols)
    spare_slots = (array(SPARE, channels, cols),) * partners

    def hbm(value):
        return pltpu.with_memory_space_constraint(value, pltpu.HBM)

    row_blocks, *edges = call(
        functools.partial(prepare_kernel, bands),
        (array(rows, channels, cols),) + edge,
        [whole(pltpu.HBM)],
        (whole(VMEM),) * (1 + edge_count),
        [
            VMEM((channels * rows, cols), BF16),
            VMEM((channels * rows, cols), F32),
            pltpu.SemaphoreType.DMA((channels // 16,)),
        ],
        "prepare",
    )(hbm(fields.reshape(channels * rows, cols)))
    before, after = swap_lat(edges, bands)

    send_rows = call(
        functools.partial(send_kernel, tiles, rows, per_row),
        array(tiles * STRIDE, dtype=jnp.int32),
        [whole(SMEM)] * 2,
        whole(SMEM),
        (),
        "send",
    )(lists, number)
    ext_blocks, *rest = call(
        functools.partial(pack_kernel, tiles, width),
        (array(ext + 1, channels, cols),) + base_slots + (half_slots,) * PARTS + spare_slots,
        [whole(SMEM)] + [whole(VMEM)] * 3,
        (whole(VMEM),) * (2 * partners + PARTS),
        (),
        "pack",
    )(send_rows, row_blocks, before, after)
    base, halves, spare = (
        rest[: partners - 1],
        rest[partners - 1 : partners - 1 + PARTS],
        rest[partners - 1 + PARTS :],
    )
    halves = [move(half, middle) for half in halves]
    base = move_whole(base, 1)

    mixing = weights.reshape(rows, per_row, taps, cols).astype(F32)
    mixing = jnp.transpose(mixing, (2, 0, 1, 3)).reshape(taps, entries, cols)
    cot_rows, mix, places, own_table, needed = call(
        functools.partial(arrival_kernel, tiles, per_row),
        (
            array(rows, channels, cols),
            array(taps, entries, cols, dtype=F32),
            array(2 * entries + tiles, dtype=jnp.int32),
            array(STRIDE, dtype=jnp.int32),
            array(1, dtype=jnp.int32),
        ),
        [whole(SMEM)] * 3 + [whole(VMEM)] * 2,
        (whole(VMEM), whole(VMEM), whole(SMEM), whole(SMEM), whole(SMEM)),
        [VMEM((channels * rows, cols), F32), SMEM((tiles + 1,), jnp.int32)],
        "arrival",
    )(send_rows, lists, number, arrival_cot.reshape(channels * rows, cols), mixing)
    if tiles <= 4:
        needed = needed[0] > 0
    else:
        tile = jnp.arange(tiles, dtype=jnp.int32)
        entry = jnp.arange(per_row, dtype=jnp.int32)
        named = (entry[:, None] < number[0][:, None, :]) & (lists[0, :, 0] == tile[:, None, None, None])
        filled = jnp.sum(jnp.where(named, 1, 0), axis=(2, 3))
        needed = jnp.any((filled > BASE) & (tile[None, :] != tile[:, None]))
    spare = move_spare(list(lax.optimization_barrier((*spare, halves[0], base[0]))[:partners]), 1)

    filling = (array(CAP, channels, cols),) + base_slots + spare_slots
    began, back, partial = [], [], []
    for i in range(PARTS):
        inputs = 4 + 2 * partners
        *began, half, sums = call(
            functools.partial(compute_kernel, tiles, per_row, i * width, width),
            filling + (half_slots, array(entries * taps, 8, cols, dtype=F32)),
            [whole(SMEM)] + [whole(VMEM)] * (inputs - 1 + len(began)),
            (whole(VMEM),) * (len(filling) + 2),
            [
                VMEM((tiles * STRIDE + ext + 1, width, cols), BF16),
                VMEM((tiles * STRIDE + 1, width, cols), BF16),
            ],
            "compute",
            {inputs + j: j for j in range(len(began))},
        )(places, mix, cot_rows, ext_blocks, *base, halves[i], *spare, *began)
        back.append(move(half, -middle))
        partial.append(sums)
    own, base, spare = began[0], move_whole(began[1:partners], -1), move_spare(list(lax.optimization_barrier((*began[partners:], back[0], back[-1]))[:partners]), -1)

    sums = array(ext + 1, channels, cols, dtype=F32)
    total = call(add_own_kernel, sums, [whole(SMEM), whole(VMEM)], whole(VMEM), (), "add_own")(
        own_table, own
    )
    returned = [*base, *back, *spare]
    edges = call(
        functools.partial(edge_kernel, tiles, bands),
        edge,
        [whole(SMEM)] + [whole(VMEM)] * (1 + len(returned)),
        (whole(VMEM),) * edge_count,
        [VMEM((edge_count, HR, channels, cols), F32)],
        "edges",
    )(send_rows, total, *returned)
    from_above, from_below = swap_lat(edges, bands)
    total = call(
        functools.partial(add_kernel, tiles),
        sums,
        [whole(SMEM)] + [whole(VMEM)] * (1 + len(returned)),
        whole(VMEM),
        (),
        "add",
        {1: 0},
    )(send_rows, lax.optimization_barrier((total, edges[0]))[0], *returned)
    source = call(
        functools.partial(finish_kernel, bands, rows),
        array(channels * rows, cols, dtype=F32),
        [whole(VMEM)] * 3,
        whole(pltpu.HBM),
        [VMEM((channels * rows, cols), F32), pltpu.SemaphoreType.DMA((channels // 16,))],
        "finish",
    )(total, from_above, from_below)

    *partial, _ = lax.optimization_barrier((*partial, edges[0]))
    weight_grad = call(
        gradient_kernel,
        array(entries * taps, cols),
        [whole(VMEM)] * PARTS,
        whole(VMEM),
        (),
        "gradient",
    )(*partial)
    return source.reshape(fields.shape), weight_grad.reshape(weights.shape)


def solution(mesh):
    return jax.shard_map(
        local,
        mesh=mesh,
        in_specs=(
            P("lev", "ens", "lat", "lon"),
            P("lev", "ens", "lat", "lon"),
            P("lev", "lat", "lon", "ens", None, None),
            P("lev", "lat", None, "ens", None),
            P("lev", "lat", "ens"),
        ),
        out_specs=(P("lev", "ens", "lat", "lon"), P("lev", "lat", "lon", "ens", None, None)),
        check_vma=False,
    )
```

```python
import functools

import jax
import jax.numpy as jnp
from jax import lax
from jax.experimental import pallas as pl
from jax.experimental.pallas import tpu as pltpu
from jax.sharding import PartitionSpec as P

HR = 2
CAP = 11
BASE = 8
SPARE = CAP - BASE
PARTS = 1
STRIDE = 16
TRASH = STRIDE - 2
COUNT = STRIDE - 1
BF16 = jnp.bfloat16
F32 = jnp.float32
VMEM = pltpu.VMEM
SMEM = pltpu.SMEM


def whole(space):
    return pl.BlockSpec(memory_space=space)


def wrap(value, size):
    return jnp.where(value < 0, value + size, value)


def prepare_kernel(bands, fields_hbm, rows_ref, *rest):
    *edges, held, wide, sems = rest
    rows, channels, _ = rows_ref.shape
    chunk = 16
    copies = []
    for i, c in enumerate(range(0, channels, chunk)):
        span = pl.ds(c * rows, chunk * rows)
        copies.append(pltpu.make_async_copy(fields_hbm.at[span], held.at[span], sems.at[i]))
        copies[-1].start()
    for i, c in enumerate(range(0, channels, chunk)):
        copies[i].wait()
        span = slice(c * rows, (c + chunk) * rows)
        wide[span] = held[span].astype(F32)
        for r in range(rows):
            rows_ref[r, c : c + chunk] = wide[pl.ds(c * rows + r, chunk, stride=rows), :].astype(BF16)
    if bands == 2:
        start = jnp.where(lax.axis_index("lat") == 0, rows - HR, 0)
        edges[0][...] = rows_ref[pl.ds(start, HR)]
    else:
        edges[0][...] = rows_ref[0:HR]
        edges[1][...] = rows_ref[rows - HR : rows]


def entry_of(lists_ref, number_ref, a, r, k, rows):
    used = k < number_ref[0, a, r]
    owner = jnp.where(used, lists_ref[0, a, 0, k, r], -1)
    return owner, HR + lists_ref[0, a, 1, k, r] * rows + lists_ref[0, a, 2, k, r]


def add_up(owner, counts):
    return [count + jnp.where(owner == o, 1, 0) for o, count in enumerate(counts)]


def send_kernel(tiles, rows, per_row, lists_ref, number_ref, send_ref):
    me = lax.axis_index("lon")

    def scan(d, most):
        a = wrap(me + d - tiles, tiles)
        for s in range(CAP):
            send_ref[d * STRIDE + s] = rows + 2 * HR
        filled = jnp.int32(0)
        others = [o for o in range(1, tiles) if o != d] if tiles <= 4 else []
        owners = [wrap(me + o - tiles, tiles) for o in others]
        counts = [jnp.int32(0)] * len(others)
        for r in range(rows):
            for k in range(per_row):
                owner, row = entry_of(lists_ref, number_ref, a, r, k, rows)
                hit = owner == me
                send_ref[d * STRIDE + jnp.where(hit, filled, TRASH)] = row
                filled = filled + jnp.where(hit, 1, 0)
                counts = [count + jnp.where(owner == o, 1, 0) for o, count in zip(owners, counts)]
        send_ref[d * STRIDE + COUNT] = filled
        for count in [filled] + counts:
            most = jnp.maximum(most, count)
        return most

    if tiles <= 4:
        most = jnp.int32(0)
        for d in range(1, tiles):
            most = scan(d, most)
        send_ref[COUNT] = most
    else:

        @pl.loop(1, tiles)
        def _(d):
            scan(d, jnp.int32(0))


def pack_kernel(tiles, width, send_ref, rows_ref, before_ref, after_ref, ext_ref, *rest):
    n = tiles - 1
    middle = tiles // 2
    base, halves, spare = rest[: n - 1], rest[n - 1 : n - 1 + PARTS], rest[n - 1 + PARTS :]
    rows = rows_ref.shape[0]
    ext_ref[0:HR] = before_ref[...]
    ext_ref[HR : HR + rows] = rows_ref[...]
    ext_ref[HR + rows : HR + rows + HR] = after_ref[...]
    whole_distances = [d for d in range(1, tiles) if d != middle]
    for s in range(BASE):
        block = ext_ref[send_ref[middle * STRIDE + s]]
        for i in range(PARTS):
            halves[i][s] = block[i * width : (i + 1) * width]
    for d, out in zip(whole_distances, base):
        for s in range(BASE):
            out[s] = ext_ref[send_ref[d * STRIDE + s]]
    for d in range(1, tiles):

        @pl.when(send_ref[d * STRIDE + COUNT] > BASE)
        def _():
            for s in range(SPARE):
                spare[d - 1][s] = ext_ref[send_ref[d * STRIDE + BASE + s]]


def arrival_kernel(tiles, per_row, send_ref, lists_ref, number_ref, cot_ref, taps_ref, *rest):
    cot_rows_ref, mix_ref, place_ref, own_ref, needed_ref, wide, taken = rest
    rows, channels, cols = cot_rows_ref.shape
    me = lax.axis_index("lon")
    entries = rows * per_row
    dump = rows + 2 * HR
    for s in range(CAP):
        own_ref[s] = dump

    def place(r, k, owner, row, d, count):
        used = owner >= 0
        own = owner == me
        slot = d * STRIDE + count
        source = jnp.where(own, tiles * STRIDE + row, slot)
        place_ref[r * per_row + k] = jnp.where(used, source, tiles * STRIDE + dump)
        place_ref[entries + r * per_row + k] = jnp.where(used, slot, tiles * STRIDE)
        own_ref[jnp.where(own, count, TRASH)] = row

    if tiles <= 4:
        most = send_ref[COUNT]
        counts = [jnp.int32(0)] * tiles
        for r in range(rows):
            for k in range(per_row):
                owner, row = entry_of(lists_ref, number_ref, me, r, k, rows)
                count = sum(jnp.where(owner == o, counts[o], 0) for o in range(tiles))
                place(r, k, owner, row, wrap(me - owner, tiles), count)
                counts = add_up(owner, counts)
        for o in range(tiles):
            place_ref[2 * entries + wrap(me - o, tiles)] = counts[o]
            most = jnp.maximum(most, jnp.where(me == o, 0, counts[o]))
        needed_ref[0] = jnp.where(most > BASE, 1, 0)
    else:
        for d in range(tiles + 1):
            taken[d] = 0

        @pl.loop(0, rows)
        def _(r):
            for k in range(per_row):
                owner, row = entry_of(lists_ref, number_ref, me, r, k, rows)
                d = jnp.where(owner >= 0, wrap(me - owner, tiles), tiles)
                place(r, k, owner, row, d, taken[d])
                taken[d] = taken[d] + 1

        for d in range(tiles):
            place_ref[2 * entries + d] = taken[d]
        needed_ref[0] = 0

    wide[...] = cot_ref[...].astype(F32)
    for r in range(rows):
        cot_rows_ref[r] = wide[pl.ds(r, channels, stride=rows), :].astype(BF16)
    w0, w1, w2, w3 = (taps_ref[j] for j in range(4))
    cell = lax.broadcasted_iota(jnp.int32, w0.shape, 1)
    first, last, late = cell == 0, cell == cols - 1, cell == cols - 2
    mix_ref[0] = pltpu.roll(jnp.where(first, 0.0, w0), cols - 1, 1)
    mix_ref[1] = w1 + jnp.where(first, w0, 0.0) + jnp.where(last, w2 + w3, 0.0)
    mix_ref[2] = pltpu.roll(jnp.where(last, 0.0, w2) + jnp.where(late, w3, 0.0), 1, 1)
    mix_ref[3] = pltpu.roll(jnp.where(last | late, 0.0, w3), 2, 1)


def compute_kernel(tiles, per_row, start, width, place_ref, mix_ref, cot_ref, ext_ref, *rest):
    n = tiles - 1
    middle = tiles // 2
    whole_distances = [d for d in range(1, tiles) if d != middle]
    base, half, spare, rest = rest[: n - 1], rest[n - 1], rest[n : 2 * n], rest[2 * n :]
    if start > 0:
        rest = rest[2 * n :]
    own_out, base_out, spare_out, rest = rest[0], rest[1:n], rest[n : 2 * n], rest[2 * n :]
    half_out, grad_ref, blocks, terms = rest
    rows, _, cols = cot_ref.shape
    entries = rows * per_row
    ext = rows + 2 * HR
    part = min(width, 32)
    mine = slice(start, start + width)
    blocks[tiles * STRIDE : tiles * STRIDE + ext] = ext_ref[0:ext, mine]
    blocks[tiles * STRIDE + ext] = jnp.zeros((width, cols), BF16)
    blocks[middle * STRIDE : middle * STRIDE + BASE] = half[...]
    for d, arrived in zip(whole_distances, base):
        blocks[d * STRIDE : d * STRIDE + BASE] = arrived[:, mine]
    for d in range(1, tiles):

        @pl.when(place_ref[2 * entries + d] > BASE)
        def _():
            blocks[d * STRIDE + BASE : d * STRIDE + CAP] = spare[d - 1][:, mine]

    def row(r, _):
        source = [place_ref[r * per_row + k] for k in range(per_row)]
        target = [place_ref[entries + r * per_row + k] for k in range(per_row)]
        mix = [[mix_ref[j, pl.ds(r * per_row + k, 1), :] for j in range(4)] for k in range(per_row)]
        grads = [None] * (per_row * 4)
        for lo in range(0, width, part):
            block = [blocks[source[k], lo : lo + part].astype(F32) for k in range(per_row)]
            tap = [sum(block[k] * mix[k][j] for k in range(per_row)) for j in range(4)]
            interp = (tap[1] + pltpu.roll(tap[0], 1, 1)) + (
                pltpu.roll(tap[2], cols - 1, 1) + pltpu.roll(tap[3], cols - 2, 1)
            )
            bent = jnp.tanh(interp)
            scaled = cot_ref[r, start + lo : start + lo + part].astype(F32) * (2.0 - bent * bent)
            scaled = scaled.astype(BF16).astype(F32)
            moved = [
                pltpu.roll(scaled, cols - 1, 1),
                scaled,
                pltpu.roll(scaled, 1, 1),
                pltpu.roll(scaled, 2, 1),
            ]
            for k in range(per_row):
                term = (moved[0] * mix[k][0] + moved[1] * mix[k][1]) + (
                    moved[2] * mix[k][2] + moved[3] * mix[k][3]
                )
                terms[target[k], lo : lo + part] = term.astype(BF16)
                for j in range(4):
                    product = jnp.sum((block[k] * moved[j]).reshape(part // 8, 8, cols), axis=0)
                    grads[k * 4 + j] = product if lo == 0 else grads[k * 4 + j] + product
        for i in range(per_row * 4):
            grad_ref[r * per_row * 4 + i] = grads[i]
        return 0

    lax.fori_loop(0, rows, row, 0, unroll=4)
    half_out[...] = terms[middle * STRIDE : middle * STRIDE + BASE]
    for d, out in zip(whole_distances, base_out):
        out[:, mine] = terms[d * STRIDE : d * STRIDE + BASE]
    for d in range(1, tiles):

        @pl.when(place_ref[2 * entries + d] > BASE)
        def _():
            spare_out[d - 1][:, mine] = terms[d * STRIDE + BASE : d * STRIDE + CAP]

    own_out[:, mine] = terms[0:CAP]


def gradient_kernel(*refs):
    *partial_refs, out_ref = refs
    sums = jnp.sum(sum(ref[...] for ref in partial_refs), axis=1)
    count, cols = sums.shape
    tap = lax.broadcasted_iota(jnp.int32, sums.shape, 0) & 3
    cell = lax.broadcasted_iota(jnp.int32, sums.shape, 1)
    grads = jnp.where(tap == 0, pltpu.roll(sums, 1, 1), sums)
    grads = jnp.where(tap == 2, pltpu.roll(sums, cols - 1, 1), grads)
    grads = jnp.where(tap == 3, pltpu.roll(sums, cols - 2, 1), grads)
    following = pltpu.roll(grads, count - 1, 0)
    previous = pltpu.roll(grads, 1, 0)
    second = pltpu.roll(grads, 2, 0)
    fixed = jnp.where((tap == 0) & (cell == 0), following, grads)
    fixed = jnp.where((tap == 2) & (cell == cols - 1), previous, fixed)
    fixed = jnp.where((tap == 3) & (cell == cols - 2), previous, fixed)
    fixed = jnp.where((tap == 3) & (cell == cols - 1), second, fixed)
    out_ref[...] = fixed.astype(BF16)


def edge_starts(bands, ext):
    if bands == 2:
        return [jnp.where(lax.axis_index("lat") == 0, ext - HR, 0)]
    return [0, ext - HR]


def add_own_kernel(tiles, bands, table_ref, send_ref, own_ref, total_ref, mask_ref):
    total_ref[...] = jnp.zeros_like(total_ref)
    for s in range(CAP):
        at = table_ref[s]
        total_ref[at] = total_ref[at] + own_ref[s].astype(F32)
    for e, start in enumerate(edge_starts(bands, total_ref.shape[0] - 1)):
        for d in range(1, tiles):
            for s in range(CAP):
                row = send_ref[d * STRIDE + s] - start
                for h in range(HR):
                    hit = jnp.where(row == h, 1.0, 0.0)
                    mask_ref[e * HR + h, (d - 1) * CAP + s] = jnp.full(mask_ref.shape[2:], hit, F32)


def slot_refs(tiles, base, halves, spare):
    middle = tiles // 2
    whole_distances = [d for d in range(1, tiles) if d != middle]
    out = [(d, 0, BASE, 0, ref) for d, ref in zip(whole_distances, base)]
    width = halves[0].shape[1]
    out += [(middle, 0, BASE, i * width, ref) for i, ref in enumerate(halves)]
    return out, [(d, BASE, SPARE, 0, ref) for d, ref in enumerate(spare, 1)]


def edge_kernel(tiles, bands, mask_ref, total_ref, *rest):
    n = tiles - 1
    base, halves, rest = rest[: n - 1], rest[n - 1 : n - 1 + PARTS], rest[n - 1 + PARTS :]
    spare, edges = rest[:n], rest[n:]
    starts = edge_starts(bands, total_ref.shape[0] - 1)
    always, seldom = slot_refs(tiles, base, halves, spare)
    _, channels, cols = edges[0].shape
    chunk = 16
    for c in range(0, channels, chunk):
        found = [
            [total_ref[start + h, c + g : c + g + 8] for g in range(0, chunk, 8)]
            for start in starts
            for h in range(HR)
        ]
        for d, first, slots, channel, ref in always + seldom:
            if not channel <= c < channel + ref.shape[1]:
                continue
            for s in range(slots):
                value = ref[s, c - channel : c - channel + chunk].astype(F32)
                for i in range(len(found)):
                    hit = mask_ref[i, (d - 1) * CAP + first + s] > 0.5
                    found[i] = [
                        group + jnp.where(hit, value[8 * g : 8 * g + 8], 0.0) for g, group in enumerate(found[i])
                    ]
        for i, groups in enumerate(found):
            edges[i // HR][i % HR, c : c + chunk] = jnp.concatenate(groups, axis=0).astype(BF16)


def add_kernel(tiles, send_ref, _, *rest):
    n = tiles - 1
    base, halves, spare, (total_ref,) = rest[: n - 1], rest[n - 1 : n - 1 + PARTS], rest[n - 1 + PARTS : 2 * n - 1 + PARTS], rest[2 * n - 1 + PARTS :]
    always, seldom = slot_refs(tiles, base, halves, spare)

    def gather(d, first, slots, channel, ref):
        part = slice(channel, channel + ref.shape[1])
        for s in range(slots):
            at = send_ref[d * STRIDE + first + s]
            total_ref[at, part] = total_ref[at, part] + ref[s].astype(F32)

    for item in always:
        gather(*item)
    for item in seldom:
        pl.when(send_ref[item[0] * STRIDE + COUNT] > BASE)(functools.partial(gather, *item))


def finish_kernel(bands, rows, total_ref, above_ref, below_ref, out_hbm, held, sems):
    channels = total_ref.shape[1]
    band = lax.axis_index("lat")
    chunk = 16
    copies = []
    for i, c in enumerate(range(0, channels, chunk)):
        part = slice(c, c + chunk)
        for r in range(rows):
            value = total_ref[HR + r, part]
            if r < HR:
                value = value + jnp.where(band > 0, above_ref[r, part].astype(F32), 0.0)
            if r >= rows - HR:
                below = below_ref[r - rows + HR, part].astype(F32)
                value = value + jnp.where(band < bands - 1, below, 0.0)
            held[pl.ds(c * rows + r, chunk, stride=rows), :] = value
        source = held.at[pl.ds(c * rows, chunk * rows)]
        target = out_hbm.at[pl.ds(c * rows, chunk * rows)]
        copies.append(pltpu.make_async_copy(source, target, sems.at[i]))
        copies[-1].start()
    for copy in copies:
        copy.wait()


def swap_lat(edges, bands):
    if bands == 2:
        got = lax.ppermute(edges[0], "lat", [(0, 1), (1, 0)])
        return got, got
    down = [(i, i + 1) for i in range(bands - 1)]
    up = [(i + 1, i) for i in range(bands - 1)]
    return lax.ppermute(edges[1], "lat", down), lax.ppermute(edges[0], "lat", up)


def local(fields, arrival_cot, weights, departures, counts):
    lev_dev, field_count, rows, cols = fields.shape
    channels = lev_dev * field_count
    tiles = lax.axis_size("lon")
    bands = lax.axis_size("lat")
    per_row, taps = weights.shape[3], weights.shape[4]
    entries = rows * per_row
    ext = rows + 2 * HR
    partners = tiles - 1
    middle = tiles // 2
    whole_distances = [d for d in range(1, tiles) if d != middle]
    width = channels // PARTS
    params = pltpu.CompilerParams(vmem_limit_bytes=48 * 1024 * 1024)

    def call(kernel, out_shape, in_specs, out_specs, scratch=(), name=None, aliases={}):
        return pl.pallas_call(
            kernel,
            out_shape=out_shape,
            in_specs=in_specs,
            out_specs=out_specs,
            scratch_shapes=list(scratch),
            compiler_params=params,
            input_output_aliases=aliases,
            name=name,
        )

    def array(*shape, dtype=BF16):
        return jax.ShapeDtypeStruct(shape, dtype)

    def move(part, d):
        return lax.ppermute(part, "lon", [(i, (i + d) % tiles) for i in range(tiles)])

    def move_all(parts, sign):
        return [move(part, sign * d) for d, part in enumerate(parts, 1)]

    def move_spare(parts, sign):
        return lax.cond(needed, lambda parts: move_all(parts, sign), lambda parts: parts, list(parts))

    def move_whole(parts, sign):
        return [move(part, sign * d) for d, part in zip(whole_distances, parts)]

    lists = jnp.transpose(departures, (0, 2, 4, 3, 1))
    number = jnp.transpose(counts, (0, 2, 1))

    edge_count = 1 if bands == 2 else 2
    edge = (array(HR, channels, cols),) * edge_count
    base_slots = (array(BASE, channels, cols),) * (partners - 1)
    half_slots = array(BASE, width, cols)
    spare_slots = (array(SPARE, channels, cols),) * partners

    def hbm(value):
        return pltpu.with_memory_space_constraint(value, pltpu.HBM)

    row_blocks, *edges = call(
        functools.partial(prepare_kernel, bands),
        (array(rows, channels, cols),) + edge,
        [whole(pltpu.HBM)],
        (whole(VMEM),) * (1 + edge_count),
        [
            VMEM((channels * rows, cols), BF16),
            VMEM((channels * rows, cols), F32),
            pltpu.SemaphoreType.DMA((channels // 16,)),
        ],
        "prepare",
    )(hbm(fields.reshape(channels * rows, cols)))
    before, after = swap_lat(edges, bands)

    send_rows = call(
        functools.partial(send_kernel, tiles, rows, per_row),
        array(tiles * STRIDE, dtype=jnp.int32),
        [whole(SMEM)] * 2,
        whole(SMEM),
        (),
        "send",
    )(lists, number)
    ext_blocks, *rest = call(
        functools.partial(pack_kernel, tiles, width),
        (array(ext + 1, channels, cols),) + base_slots + (half_slots,) * PARTS + spare_slots,
        [whole(SMEM)] + [whole(VMEM)] * 3,
        (whole(VMEM),) * (2 * partners + PARTS),
        (),
        "pack",
    )(send_rows, row_blocks, before, after)
    base, halves, spare = (
        rest[: partners - 1],
        rest[partners - 1 : partners - 1 + PARTS],
        rest[partners - 1 + PARTS :],
    )
    halves = [move(half, middle) for half in halves]
    base = move_whole(base, 1)

    mixing = weights.reshape(rows, per_row, taps, cols).astype(F32)
    mixing = jnp.transpose(mixing, (2, 0, 1, 3)).reshape(taps, entries, cols)
    cot_rows, mix, places, own_table, needed = call(
        functools.partial(arrival_kernel, tiles, per_row),
        (
            array(rows, channels, cols),
            array(taps, entries, cols, dtype=F32),
            array(2 * entries + tiles, dtype=jnp.int32),
            array(STRIDE, dtype=jnp.int32),
            array(1, dtype=jnp.int32),
        ),
        [whole(SMEM)] * 3 + [whole(VMEM)] * 2,
        (whole(VMEM), whole(VMEM), whole(SMEM), whole(SMEM), whole(SMEM)),
        [VMEM((channels * rows, cols), F32), SMEM((tiles + 1,), jnp.int32)],
        "arrival",
    )(send_rows, lists, number, arrival_cot.reshape(channels * rows, cols), mixing)
    if tiles <= 4:
        needed = needed[0] > 0
    else:
        tile = jnp.arange(tiles, dtype=jnp.int32)
        entry = jnp.arange(per_row, dtype=jnp.int32)
        named = (entry[:, None] < number[0][:, None, :]) & (lists[0, :, 0] == tile[:, None, None, None])
        filled = jnp.sum(jnp.where(named, 1, 0), axis=(2, 3))
        needed = jnp.any((filled > BASE) & (tile[None, :] != tile[:, None]))
    spare = move_spare(list(lax.optimization_barrier((*spare, halves[0], base[0]))[:partners]), 1)

    filling = (array(CAP, channels, cols),) + base_slots + spare_slots
    began, back, partial = [], [], []
    for i in range(PARTS):
        inputs = 4 + 2 * partners
        *began, half, sums = call(
            functools.partial(compute_kernel, tiles, per_row, i * width, width),
            filling + (half_slots, array(entries * taps, 8, cols, dtype=F32)),
            [whole(SMEM)] + [whole(VMEM)] * (inputs - 1 + len(began)),
            (whole(VMEM),) * (len(filling) + 2),
            [
                VMEM((tiles * STRIDE + ext + 1, width, cols), BF16),
                VMEM((tiles * STRIDE + 1, width, cols), BF16),
            ],
            "compute",
            {inputs + j: j for j in range(len(began))},
        )(places, mix, cot_rows, ext_blocks, *base, halves[i], *spare, *began)
        back.append(move(half, -middle))
        partial.append(sums)
    own, base, spare = began[0], move_whole(began[1:partners], -1), move_spare(list(lax.optimization_barrier((*began[partners:], back[0], back[-1]))[:partners]), -1)

    sums = array(ext + 1, channels, cols, dtype=F32)
    total, masks = call(
        functools.partial(add_own_kernel, tiles, bands),
        (sums, array(edge_count * HR, partners * CAP, 8, cols, dtype=F32)),
        [whole(SMEM), whole(SMEM), whole(VMEM)],
        (whole(VMEM),) * 2,
        (),
        "add_own",
    )(own_table, send_rows, own)
    returned = [*base, *back, *spare]
    edges = call(
        functools.partial(edge_kernel, tiles, bands),
        edge,
        [whole(VMEM)] * (2 + len(returned)),
        (whole(VMEM),) * edge_count,
        (),
        "edges",
    )(masks, total, *returned)
    from_above, from_below = swap_lat(edges, bands)
    total = call(
        functools.partial(add_kernel, tiles),
        sums,
        [whole(SMEM)] + [whole(VMEM)] * (1 + len(returned)),
        whole(VMEM),
        (),
        "add",
        {1: 0},
    )(send_rows, lax.optimization_barrier((total, edges[0]))[0], *returned)
    source = call(
        functools.partial(finish_kernel, bands, rows),
        array(channels * rows, cols, dtype=F32),
        [whole(VMEM)] * 3,
        whole(pltpu.HBM),
        [VMEM((channels * rows, cols), F32), pltpu.SemaphoreType.DMA((channels // 16,))],
        "finish",
    )(total, from_above, from_below)

    *partial, _ = lax.optimization_barrier((*partial, edges[0]))
    weight_grad = call(
        gradient_kernel,
        array(entries * taps, cols),
        [whole(VMEM)] * PARTS,
        whole(VMEM),
        (),
        "gradient",
    )(*partial)
    return source.reshape(fields.shape), weight_grad.reshape(weights.shape)


def solution(mesh):
    return jax.shard_map(
        local,
        mesh=mesh,
        in_specs=(
            P("lev", "ens", "lat", "lon"),
            P("lev", "ens", "lat", "lon"),
            P("lev", "lat", "lon", "ens", None, None),
            P("lev", "lat", None, "ens", None),
            P("lev", "lat", "ens"),
        ),
        out_specs=(P("lev", "ens", "lat", "lon"), P("lev", "lat", "lon", "ens", None, None)),
        check_vma=False,
    )
```
